128 devices in a mesh: gx: 4 (over y), gy: 32 (over z, x, core).
Axes of the slice: x: 4, y: 4, z: 4, core: 2. Of those that a mesh axis runs over, the one named last changes fastest.
Arguments:
- grid_latent: bfloat16 [32768, 512], P(('gx', 'gy')), may hold values from -6 to 6
- mesh_latent: bfloat16 [16384, 512], P(('gx', 'gy')), may hold values from -6 to 6
- w_grid: bfloat16 [512, 512], replicated, may hold values from -0.25 to 0.25
- w_recv: bfloat16 [512, 512], replicated, may hold values from -0.25 to 0.25
- w_send: bfloat16 [512, 512], replicated, may hold values from -0.25 to 0.25
- w_node: bfloat16 [512, 512], replicated, may hold values from -0.25 to 0.25
- encode_sender: int32 [49152], P(('gx', 'gy')), may hold values from 0 to 255
- encode_owner: int32 [49152, 1], P(('gx', 'gy')), may hold values from 0 to 127; in each aligned block of 384 rows (0 to 383, 384 to 767, ...) at most 9 rows name the same one
- encode_target: int32 [49152], P(('gx', 'gy')), may hold values from 0 to 127
- mesh_sender: int32 [65536], P(('gx', 'gy')), may hold values from 0 to 127
- mesh_owner: int32 [65536, 1], P(('gx', 'gy')), may hold values from 0 to 127; in each aligned block of 512 rows (0 to 511, 512 to 1023, ...) at most 12 rows name the same one
- mesh_target: int32 [65536], P(('gx', 'gy')), may hold values from 0 to 127
- cotangent: bfloat16 [16384, 512], P(('gx', 'gy')), may hold values from -6 to 6
Outputs:
- mesh_out: bfloat16 [16384, 512], P(('gx', 'gy'))
- grid_grad: bfloat16 [32768, 512], P(('gx', 'gy'))
- mesh_grad: bfloat16 [16384, 512], P(('gx', 'gy'))
The draws below stay inside these ranges and needn't reach their ends.
Inputs may be any that keep to these rules, and one draw needn't show every extreme that they name: `encode_owner`: in the edges of one device, at most 9 name one owner, and some device names some owner exactly 9 times. `mesh_owner`: in the edges of one device, at most 12 name one owner, and some device names some owner exactly 12 times.
All inputs are finite; a program needn't handle non-finite values.
Results may differ from the reference program's by a relative error of at most 0.02.
Values may be sent and summed in bfloat16 or wider, within the bound.
A program may use at most 128 MiB of HBM per device.

```python
import math
import jax
import jax.numpy as jnp
import numpy as np
from jax import lax

D = 512
G_DEV = 256
M_DEV = 128
ENC_DEV = 384
MSH_DEV = 512
ENC_CAP = 9
MSH_CAP = 12
GRID = 32768
MESH = 16384
ENC_EDGES = 49152
MSH_EDGES = 65536
DEVICES = 128


def with_ends(values, key, least, largest):
    extent = values.shape
    spot = [jax.random.randint(jax.random.fold_in(key, axis), (), 0, extent[axis]) for axis in range(len(extent))]
    values = values.at[tuple(spot)].set(least)
    longest = extent.index(max(extent))
    spot[longest] = (spot[longest] + 1) % extent[longest]
    return values.at[tuple(spot)].set(largest)


def block_levels(key, dims, pieces, smallest, high):
    def one(position, parts):
        heights = jax.random.uniform(jax.random.fold_in(jax.random.fold_in(key, 6), position), (parts,), jnp.float32, smallest / len(pieces), high / len(pieces))
        return jnp.repeat(jnp.exp(heights), dims[position] // parts).reshape((-1,) + (1,) * (len(dims) - position - 1))

    factor_of = one(*pieces[0])
    for cut in pieces[1:]:
        factor_of = factor_of * one(*cut)
    return factor_of


def deal_out(own_key, own, number, rows, count, top, most, slope):
    ranking = jax.random.permutation(own_key, count)
    packed, usual = shares(count, rows * top, most, slope, True), shares(count, rows * top, most, slope, False)
    places = jnp.arange(count)

    def named(sizes, rotation):
        used = int((sizes > 0).sum())
        fixed = max(1, used // 4)
        passed = fixed + (places - fixed + rotation * (used - fixed)) % max(1, count - fixed)
        return jnp.zeros((count,), jnp.int32).at[ranking[jnp.where(places < fixed, places, passed)]].set(jnp.asarray(sizes, jnp.int32))

    sizes = jnp.where(number % 4 == 0, named(packed, number // 4), named(usual, number - number // 4 - 1))
    mixed = jax.random.permutation(jax.random.fold_in(own, 3), count)
    donor, sink = mixed[0:count // 2 * 2:2], mixed[1:count // 2 * 2:2]
    margin = jnp.minimum(sizes[donor] - 1, most - sizes[sink]) // 2
    margin = jnp.where((donor == ranking[0]) | (sink == ranking[0]) | (sizes[sink] == 0), 0, jnp.maximum(margin, 0))
    passed = jax.random.randint(jax.random.fold_in(own, 4), (count // 2,), 0, 1 << 20) % (margin + 1)
    sizes = sizes.at[donor].add(-passed).at[sink].add(passed)
    labels = jnp.searchsorted(jnp.cumsum(sizes), jnp.arange(rows * top), side="right").astype(jnp.int32)
    table = labels.reshape(top, rows).T
    table = table[jax.random.permutation(jax.random.fold_in(own, 1), rows)]
    rotation = jax.random.randint(jax.random.fold_in(own, 2), (rows, 1), 0, top)
    return jnp.take_along_axis(table, (jnp.arange(top)[None, :] + rotation) % top, axis=1)


def shares(number_of, total, limit, slope, full):
    weights = [(1 << 20) // math.isqrt(standing ** slope) + 1 for standing in range(1, number_of + 1)]
    largest = limit if full else min(limit, max(-(-total // number_of), total * weights[0] // sum(weights)))
    least = 1 if total - largest >= number_of - 1 else 0
    given, surplus = [largest] + [least] * (number_of - 1), total - largest - least * (number_of - 1)
    while surplus > 0:
        movable = [i for i in range(1, number_of) if given[i] < largest] or [i for i in range(1, number_of) if given[i] < limit]
        pool, remaining = sum([weights[i] for i in movable]), surplus
        for i in movable:
            more = min(limit - given[i], max(1, remaining * weights[i] // pool), surplus)
            given[i] = given[i] + more
            surplus = surplus - more
    return np.array(given)


def centred(rng, dims, spread, bound, split=(), kind=jnp.bfloat16):
    entries = spread * jax.random.normal(rng, dims, jnp.float32)
    if split:
        entries = entries * block_levels(rng, dims, split, -0.22, 0.18)
    return jnp.clip(entries, -bound, bound).astype(kind)


def setup_inputs(seed: int = 0) -> dict:
    keys = jax.random.split(jax.random.key(seed), 14)
    grid_latent = centred(keys[0], (GRID, D), 1.0, 6.0, ((0, 128),))
    mesh_latent = centred(keys[1], (MESH, D), 1.0, 6.0, ((0, 128),))
    w_grid = centred(keys[2], (D, D), D ** -0.5, 0.25)
    w_recv = centred(keys[3], (D, D), D ** -0.5, 0.25)
    w_send = centred(keys[4], (D, D), D ** -0.5, 0.25)
    w_node = centred(keys[5], (D, D), D ** -0.5, 0.25)
    encode_sender = with_ends(jax.random.randint(keys[6], (ENC_EDGES,), 0, G_DEV), jax.random.fold_in(keys[6], 1), 0, G_DEV - 1).astype(jnp.int32)
    encode_owner_keys = jax.random.split(jax.random.fold_in(keys[7], 1), ENC_EDGES // ENC_DEV)
    encode_owner_turns = jax.random.permutation(jax.random.fold_in(keys[7], 3), ENC_EDGES // ENC_DEV)
    encode_owner = jax.vmap(lambda own, number: deal_out(jax.random.fold_in(keys[7], 2), own, number, ENC_DEV, DEVICES, 1, ENC_CAP, 2))(encode_owner_keys, encode_owner_turns).reshape((ENC_EDGES, 1))
    encode_target = with_ends(jax.random.randint(keys[8], (ENC_EDGES,), 0, M_DEV), jax.random.fold_in(keys[8], 1), 0, M_DEV - 1).astype(jnp.int32)
    mesh_sender = with_ends(jax.random.randint(keys[9], (MSH_EDGES,), 0, M_DEV), jax.random.fold_in(keys[9], 1), 0, M_DEV - 1).astype(jnp.int32)
    mesh_owner_keys = jax.random.split(jax.random.fold_in(keys[10], 1), MSH_EDGES // MSH_DEV)
    mesh_owner_turns = jax.random.permutation(jax.random.fold_in(keys[10], 3), MSH_EDGES // MSH_DEV)
    mesh_owner = jax.vmap(lambda own, number: deal_out(jax.random.fold_in(keys[10], 2), own, number, MSH_DEV, DEVICES, 1, MSH_CAP, 2))(mesh_owner_keys, mesh_owner_turns).reshape((MSH_EDGES, 1))
    mesh_target = with_ends(jax.random.randint(keys[11], (MSH_EDGES,), 0, M_DEV), jax.random.fold_in(keys[11], 1), 0, M_DEV - 1).astype(jnp.int32)
    cotangent = centred(keys[12], (MESH, D), 1.0, 6.0, ((0, 128),))
    return dict(grid_latent=grid_latent, mesh_latent=mesh_latent, w_grid=w_grid, w_recv=w_recv, w_send=w_send, w_node=w_node, encode_sender=encode_sender, encode_owner=encode_owner, encode_target=encode_target, mesh_sender=mesh_sender, mesh_owner=mesh_owner, mesh_target=mesh_target, cotangent=cotangent)


def rms_norm(values):
    return values * lax.rsqrt(lax.optimization_barrier(jnp.mean(values * values, axis=-1, keepdims=True)) + 1e-05)

def reference(grid_latent, mesh_latent, w_grid, w_recv, w_send, w_node, encode_sender, encode_owner, encode_target, mesh_sender, mesh_owner, mesh_target, cotangent):
    enc_block = (jnp.arange(ENC_EDGES) // ENC_DEV).astype(jnp.int32)
    enc_source = enc_block * G_DEV + encode_sender
    enc_dest = encode_owner[:, 0] * M_DEV + encode_target
    msh_block = (jnp.arange(MSH_EDGES) // MSH_DEV).astype(jnp.int32)
    msh_source = msh_block * M_DEV + mesh_sender
    msh_dest = mesh_owner[:, 0] * M_DEV + mesh_target
    both_weights = jnp.concatenate([w_send, w_recv], axis=1)

    def forward(grid_values, mesh_values):
        grid_proj = jnp.dot(grid_values, w_grid, preferred_element_type=jnp.float32)
        enc_rows = grid_proj[enc_source].astype(jnp.bfloat16)
        recv_proj = jnp.dot(mesh_values, w_recv, preferred_element_type=jnp.float32)
        enc_msg = jax.nn.silu(enc_rows.astype(jnp.float32) + recv_proj[enc_dest]).astype(jnp.bfloat16)
        enc_sum = jax.ops.segment_sum(enc_msg.astype(jnp.float32), enc_dest, num_segments=MESH)
        enc_norm = rms_norm(enc_sum).astype(jnp.bfloat16)
        hidden = mesh_values.astype(jnp.float32) + jnp.dot(enc_norm, w_node, preferred_element_type=jnp.float32)
        hidden_bf = hidden.astype(jnp.bfloat16)
        projected = jnp.dot(hidden_bf, both_weights, preferred_element_type=jnp.float32)
        send_proj = projected[:, :D]
        recv_next = projected[:, D:]
        msh_rows = send_proj[msh_source].astype(jnp.bfloat16)
        msh_msg = jax.nn.silu(msh_rows.astype(jnp.float32) + recv_next[msh_dest]).astype(jnp.bfloat16)
        msh_sum = jax.ops.segment_sum(msh_msg.astype(jnp.float32), msh_dest, num_segments=MESH)
        msh_norm = rms_norm(msh_sum).astype(jnp.bfloat16)
        return (hidden + jnp.dot(msh_norm, w_node, preferred_element_type=jnp.float32)).astype(jnp.bfloat16)
    mesh_out, pullback = jax.vjp(forward, grid_latent, mesh_latent)
    grid_grad, mesh_grad = pullback(cotangent)
    return (mesh_out, grid_grad, mesh_grad)
```

```python
import functools

import jax
import jax.numpy as jnp
from jax import lax
from jax.experimental import pallas as pl
from jax.experimental.pallas import tpu as pltpu
from jax.sharding import PartitionSpec as P

MESH = pl.DeviceIdType.MESH
BF = jnp.bfloat16
F32 = jnp.float32
I32 = jnp.int32

PEERS = 128
GROUPS = 8
SIZE = 16
MAIN = SIZE * 8
TAIL = SIZE * 4
ROWS = MAIN + TAIL
UNITS = 48
FORTH, BACK = 37, 45


def coords():
    y = lax.axis_index("gx")
    g = lax.axis_index("gy")
    return y, g // 8, (g // 2) % 4, g % 2


def partner(j, sign):
    y, z, x, c = coords()
    i = (j * FORTH) % PEERS
    dy, dz, dx, dc = i // 32, (i // 8) % 4, (i // 2) % 4, i % 2
    if sign < 0:
        dy, dz, dx = 4 - dy, 4 - dz, 4 - dx
    return (y + dy) % 4, ((z + dz) % 4) * 8 + ((x + dx) % 4) * 2 + (c + dc) % 2


def iota(shape, axis):
    return lax.broadcasted_iota(I32, shape, axis)


def onehot(mask):
    return jnp.where(mask, 1.0, 0.0).astype(BF)


def mm(a, b):
    return lax.dot_general(a, b, (((1,), (0,)), ((), ())), preferred_element_type=F32)


def mm_nt(a, b):
    return lax.dot_general(a, b, (((1,), (1,)), ((), ())), preferred_element_type=F32)


def swap(a, b):
    low = iota(a.shape, 1) < 4
    return jnp.where(low, a, pltpu.roll(b, 4, 1)), jnp.where(low, pltpu.roll(a, 4, 1), b)


def pack(wire, g, rows):
    at = pl.ds(g * SIZE, SIZE)
    m = [rows[:MAIN, c * 128 : c * 128 + 128].reshape(SIZE, 8, 128) for c in range(4)]
    t = [rows[MAIN:, c * 128 : c * 128 + 128].reshape(SIZE // 2, 8, 128) for c in range(4)]
    wire[at, 0:16, :] = jnp.concatenate([m[0], m[1]], axis=1).astype(BF)
    wire[at, 16:32, :] = jnp.concatenate([m[2], m[3]], axis=1).astype(BF)
    e01, o01 = swap(t[0], t[1])
    e23, o23 = swap(t[2], t[3])
    even = jnp.concatenate([e01, e23], axis=1)
    odd = jnp.concatenate([o01, o23], axis=1)
    wire[at, 32:48, :] = jnp.stack([even, odd], axis=1).reshape(SIZE, 16, 128).astype(BF)


def unpack(wire, g):
    at = pl.ds(g * SIZE, SIZE)
    a = wire[at, 0:16, :].astype(F32)
    b = wire[at, 16:32, :].astype(F32)
    t = wire[at, 32:48, :].astype(F32).reshape(SIZE // 2, 2, 16, 128)
    even, odd = t[:, 0], t[:, 1]
    t0, t1 = swap(even[:, :8], odd[:, :8])
    t2, t3 = swap(even[:, 8:], odd[:, 8:])
    main = [v.reshape(MAIN, 128) for v in (a[:, :8], a[:, 8:], b[:, :8], b[:, 8:])]
    tail = [v.reshape(TAIL, 128) for v in (t0, t1, t2, t3)]
    return jnp.concatenate(
        [jnp.concatenate(main, axis=1), jnp.concatenate(tail, axis=1)], axis=0
    )


def norm_forward(total):
    scale = lax.rsqrt(jnp.mean(total * total, axis=-1, keepdims=True) + 1e-05)
    return total * scale, scale


def norm_backward(grad, total, scale):
    inner = jnp.mean(grad * total, axis=-1, keepdims=True)
    return scale * (grad - total * (scale * scale * inner))


def kernel(
    grid_ref,
    mesh_ref,
    w_grid,
    w_recv,
    w_send,
    w_node,
    es,
    eo,
    et,
    ms,
    mo,
    mt,
    cot,
    out_ref,
    grid_grad,
    mesh_grad,
    send1,
    recv1,
    send2,
    recv2,
    back2,
    ret2,
    back1,
    ret1,
    a1,
    a1t,
    a2,
    a2t,
    r1,
    r1t,
    r2,
    r2t,
    d1,
    d2,
    tm,
    rows1,
    gathered,
    total,
    hidden_ref,
    ssem,
    rsem,
):
    barrier = pltpu.get_barrier_semaphore()

    def signal(j, carry):
        ty, tg = partner(j, 1)
        pl.semaphore_signal(barrier, inc=1, device_id=(ty, tg), device_id_type=MESH)
        return carry

    lax.fori_loop(1, PEERS, signal, 0)

    y, z, x, c = coords()

    def route(owner):
        edges = owner.shape[1]
        dy = ((owner >> 5) - y) & 3
        dz = (((owner >> 3) & 3) - z) & 3
        dx = (((owner >> 1) & 3) - x) & 3
        dc = ((owner & 1) - c) & 1
        j = ((dy * 32 + dz * 8 + dx * 2 + dc) * BACK) & 127
        same = iota((PEERS, edges), 0) == j
        before = onehot(iota((edges, edges), 0) < iota((edges, edges), 1))
        count = mm(onehot(same), before)
        rank = jnp.sum(jnp.where(same, count, 0.0), axis=0, keepdims=True).astype(I32)
        return j, rank, onehot(same)

    def slots(j, rank):
        inside = jnp.where(rank < 8, (j & 15) * 8 + rank, MAIN + (j & 15) * 4 + rank - 8)
        return (j >> 4) * ROWS + inside

    def labels(rank, target, base):
        at = iota((128, rank.shape[1]), 0) == rank + base
        return jnp.where(at, (target + 1).astype(F32), 0.0).astype(BF)

    def selectors(place, sender, nodes, a, at):
        edges = place.shape[1]
        q = onehot(iota((nodes, edges), 0) == sender)
        for g in range(GROUPS):
            p = onehot(iota((ROWS, edges), 0) + g * ROWS == place)
            a[g] = mm_nt(p, q).astype(BF)
            at[g] = mm_nt(q, p).astype(BF)

    j1, k1, same1 = route(eo[...])
    j2, k2, same2 = route(mo[...])
    tm[...] = (
        mm_nt(same1, labels(k1, et[...], 0)) + mm_nt(same2, labels(k2, mt[...], 16))
    ).astype(BF)
    selectors(slots(j1, k1), es[...], grid_ref.shape[0], a1, a1t)
    selectors(slots(j2, k2), ms[...], mesh_ref.shape[0], a2, a2t)
    rows1[...] = mm(grid_ref[...], w_grid[...]).astype(BF)
    gathered[...] = mm(mesh_ref[...], w_recv[...]).astype(BF)

    pl.semaphore_wait(barrier, PEERS - 1)

    def send_group(g, phase, src, dst, sign):
        def one(k, carry):
            j = g * SIZE + k
            ty, tg = partner(j, sign)
            pltpu.make_async_remote_copy(
                src.at[j],
                dst.at[j],
                ssem.at[phase],
                rsem.at[phase, g],
                device_id=(ty, tg),
                device_id_type=MESH,
            ).start()
            return carry

        @pl.when(g == 0)
        def _():
            pltpu.make_async_copy(src.at[0], dst.at[0], rsem.at[phase, 0]).start()
            lax.fori_loop(1, SIZE, one, 0)

        @pl.when(g > 0)
        def _():
            lax.fori_loop(0, SIZE, one, 0)

    def wait_group(g, phase, dst):
        at = dst.at[pl.ds(g * SIZE, SIZE)]
        pltpu.make_async_copy(at, at, rsem.at[phase, g]).wait()

    slot_r = iota((ROWS, SIZE), 0)
    peer_r = iota((ROWS, SIZE), 1)
    slot_c = iota((SIZE, ROWS), 1)
    peer_c = iota((SIZE, ROWS), 0)

    def peer_of(s):
        return jnp.where(s < MAIN, s >> 3, (s - MAIN) >> 2)

    def rank_of(s):
        return jnp.where(s < MAIN, s & 7, 8 + (s & 3))

    mark = onehot((slot_r == MAIN + 4 * peer_r + 1))
    unmark = onehot((slot_c == MAIN + 4 * peer_c + 1))
    spread = onehot(peer_of(slot_c) == peer_c)
    eye128 = onehot(iota((128, 128), 0) == iota((128, 128), 1))
    eye_rows = onehot(iota((ROWS, ROWS), 0) == iota((ROWS, ROWS), 1))
    rank_c = rank_of(iota((128, ROWS), 1))
    lane_of = iota((128, ROWS), 0)

    def send_enc(g, carry):
        rows = mm(a1[g], rows1[...])
        label = mm(mark, tm[pl.ds(pl.multiple_of(g * SIZE, SIZE), SIZE), :])
        rows = jnp.concatenate([rows[:, :128] + label, rows[:, 128:]], axis=1)
        pack(send1, g, rows)
        send_group(g, 0, send1, recv1, 1)
        return carry

    lax.fori_loop(0, GROUPS, send_enc, 0)

    def message(g, rows, r, rt, d):
        pre = rows + mm(r[g], gathered[...])
        gate = 0.5 * jnp.tanh(0.5 * pre) + 0.5
        value = pre * gate
        d[g] = (gate + value * (1.0 - gate)).astype(BF)
        total[...] += mm(rt[g], value.astype(BF))

    total[...] = jnp.zeros_like(total)

    def take_enc(g, carry):
        wait_group(g, 0, recv1)
        rows = unpack(recv1, g)
        mine = mm(unmark, rows[:, :128].astype(BF)).astype(BF)
        mine_t = mm_nt(eye128, mine).astype(BF)
        lines = mm(mine_t, spread)
        for base, r, rt in ((0, r1, r1t), (16, r2, r2t)):
            row = jnp.sum(
                jnp.where(lane_of == rank_c + base, lines, 0.0), axis=0, keepdims=True
            )
            flag = onehot(row.astype(I32) == lane_of + 1)
            rt[g] = flag
            r[g] = mm_nt(eye_rows, flag).astype(BF)
        message(g, rows, r1, r1t, d1)
        return carry

    lax.fori_loop(0, GROUPS, take_enc, 0)

    enc_sum = total[...]
    enc_norm, enc_scale = norm_forward(enc_sum)
    hidden = mesh_ref[...].astype(F32) + mm(enc_norm.astype(BF), w_node[...])
    hidden_ref[...] = hidden
    hidden_bf = hidden.astype(BF)
    sent = mm(hidden_bf, w_send[...]).astype(BF)
    rows1[pl.ds(0, 128), :] = sent

    def send_msh(g, carry):
        pack(send2, g, mm(a2[g], rows1[pl.ds(0, 128), :]))
        send_group(g, 1, send2, recv2, 1)
        return carry

    lax.fori_loop(0, GROUPS, send_msh, 0)
    gathered[...] = mm(hidden_bf, w_recv[...]).astype(BF)
    total[...] = jnp.zeros_like(total)

    def take_msh(g, carry):
        wait_group(g, 1, recv2)
        message(g, unpack(recv2, g), r2, r2t, d2)
        return carry

    lax.fori_loop(0, GROUPS, take_msh, 0)

    msh_sum = total[...]
    msh_norm, msh_scale = norm_forward(msh_sum)
    cot_bf = cot[...]
    grad_norm = mm_nt(cot_bf, w_node[...]).astype(BF).astype(F32)
    gathered[...] = norm_backward(grad_norm, msh_sum, msh_scale).astype(BF)

    total[...] = jnp.zeros_like(total)

    def grad_group(g, phase, r, rt, d, back, ret):
        grad = mm(r[g], gathered[...]) * d[g].astype(F32)
        pack(back, g, grad)
        send_group(g, phase, back, ret, -1)
        total[...] += mm(rt[g], grad.astype(BF))

    def back_msh(g, carry):
        grad_group(g, 2, r2, r2t, d2, back2, ret2)
        return carry

    lax.fori_loop(0, GROUPS, back_msh, 0)
    out_ref[...] = (hidden_ref[...] + mm(msh_norm.astype(BF), w_node[...])).astype(BF)
    grad_recv = total[...].astype(BF)
    part = mm_nt(grad_recv, w_recv[...])
    total[...] = jnp.zeros_like(total)

    def take_back_msh(g, carry):
        wait_group(g, 2, ret2)
        total[...] += mm(a2t[g], unpack(ret2, g).astype(BF))
        return carry

    lax.fori_loop(0, GROUPS, take_back_msh, 0)
    grad_hidden_bf = (part + mm_nt(total[...].astype(BF), w_send[...])).astype(BF)
    grad_hidden = (cot_bf.astype(F32) + grad_hidden_bf.astype(F32)).astype(BF)
    grad_norm1 = mm_nt(grad_hidden, w_node[...]).astype(BF).astype(F32)
    gathered[...] = norm_backward(grad_norm1, enc_sum, enc_scale).astype(BF)

    total[...] = jnp.zeros_like(total)

    def back_enc(g, carry):
        grad_group(g, 3, r1, r1t, d1, back1, ret1)
        return carry

    lax.fori_loop(0, GROUPS, back_enc, 0)
    mesh_part = mm_nt(total[...].astype(BF), w_recv[...]).astype(BF)
    mesh_grad[...] = (grad_hidden.astype(F32) + mesh_part.astype(F32)).astype(BF)

    def take_back_enc(g, carry):
        wait_group(g, 3, ret1)
        return carry + mm(a1t[g], unpack(ret1, g).astype(BF))

    grid_rows = lax.fori_loop(
        0, GROUPS, take_back_enc, jnp.zeros(grid_ref.shape, F32)
    )
    grid_grad[...] = mm_nt(grid_rows.astype(BF), w_grid[...]).astype(BF)

    for phase, src in enumerate((send1, send2, back2, back1)):
        at = src.at[pl.ds(1, PEERS - 1)]
        pltpu.make_async_copy(at, at, ssem.at[phase]).wait()


def body(
    grid_latent,
    mesh_latent,
    w_grid,
    w_recv,
    w_send,
    w_node,
    encode_sender,
    encode_owner,
    encode_target,
    mesh_sender,
    mesh_owner,
    mesh_target,
    cotangent,
):
    vmem = pl.BlockSpec(memory_space=pltpu.VMEM)
    wire = pltpu.VMEM((PEERS, UNITS, 128), BF)
    nodes, width = mesh_latent.shape
    grid_nodes = grid_latent.shape[0]
    scratch = (
        [wire] * 8
        + [
            pltpu.VMEM((GROUPS, ROWS, grid_nodes), BF),
            pltpu.VMEM((GROUPS, grid_nodes, ROWS), BF),
            pltpu.VMEM((GROUPS, ROWS, nodes), BF),
            pltpu.VMEM((GROUPS, nodes, ROWS), BF),
        ]
        + [pltpu.VMEM((GROUPS, ROWS, nodes), BF), pltpu.VMEM((GROUPS, nodes, ROWS), BF)] * 2
        + [pltpu.VMEM((GROUPS, ROWS, width), BF)] * 2
        + [
            pltpu.VMEM((PEERS, 128), BF),
            pltpu.VMEM((grid_nodes, width), BF),
            pltpu.VMEM((nodes, width), BF),
            pltpu.VMEM((nodes, width), F32),
            pltpu.VMEM((nodes, width), F32),
            pltpu.SemaphoreType.DMA((4,)),
            pltpu.SemaphoreType.DMA((4, GROUPS)),
        ]
    )
    row = lambda v: v.reshape(1, -1)
    return pl.pallas_call(
        kernel,
        out_shape=(
            jax.ShapeDtypeStruct(mesh_latent.shape, BF),
            jax.ShapeDtypeStruct(grid_latent.shape, BF),
            jax.ShapeDtypeStruct(mesh_latent.shape, BF),
        ),
        in_specs=[vmem] * 13,
        out_specs=[vmem] * 3,
        scratch_shapes=scratch,
        compiler_params=pltpu.CompilerParams(
            collective_id=0, has_side_effects=True, vmem_limit_bytes=56 << 20
        ),
    )(
        grid_latent,
        mesh_latent,
        w_grid,
        w_recv,
        w_send,
        w_node,
        row(encode_sender),
        row(encode_owner),
        row(encode_target),
        row(mesh_sender),
        row(mesh_owner),
        row(mesh_target),
        cotangent,
    )


def solution(mesh):
    rows = P(("gx", "gy"), None)
    flat = P(("gx", "gy"))
    placed = (rows, rows, P(), P(), P(), P(), flat, rows, flat, flat, rows, flat, rows)
    return jax.shard_map(
        body, mesh=mesh, in_specs=placed, out_specs=(rows, rows, rows), check_vma=False
    )
```

```python
import jax
import jax.numpy as jnp
from jax import lax
from jax.experimental import pallas as pl
from jax.experimental.pallas import tpu as pltpu
from jax.sharding import PartitionSpec as P

MESH = pl.DeviceIdType.MESH
BF = jnp.bfloat16
F32 = jnp.float32
I32 = jnp.int32

PEERS = 128
GROUPS = 8
SIZE = 16
MAIN = SIZE * 8
TAIL = SIZE * 4
LAST = SIZE * 8
ROWS1 = MAIN + LAST
ROWS2 = MAIN + TAIL
NEVER = 99


def coords():
    y = lax.axis_index("gx")
    g = lax.axis_index("gy")
    return y, g // 8, (g // 2) % 4, g % 2


def iota(shape, axis):
    return lax.broadcasted_iota(I32, shape, axis)


def onehot(mask):
    return jnp.where(mask, 1.0, 0.0).astype(BF)


def mm(a, b):
    return lax.dot_general(a, b, (((1,), (0,)), ((), ())), preferred_element_type=F32)


def mm_nt(a, b):
    return lax.dot_general(a, b, (((1,), (1,)), ((), ())), preferred_element_type=F32)


def quarter(v, q):
    return v[..., q * 128 : q * 128 + 128]


def swap(a, b):
    low = iota(a.shape, 1) < 4
    return jnp.where(low, a, pltpu.roll(b, 4, 1)), jnp.where(low, pltpu.roll(a, 4, 1), b)


def pack_main(wire, g, rows):
    at = pl.ds(g * SIZE, SIZE)
    m = [quarter(rows, q).reshape(SIZE, 8, 128) for q in range(4)]
    wire[at, 0:16, :] = jnp.concatenate([m[0], m[1]], axis=1).astype(BF)
    wire[at, 16:32, :] = jnp.concatenate([m[2], m[3]], axis=1).astype(BF)


def unpack_main(wire, g):
    at = pl.ds(g * SIZE, SIZE)
    a = wire[at, 0:16, :].astype(F32)
    b = wire[at, 16:32, :].astype(F32)
    parts = (a[:, :8], a[:, 8:], b[:, :8], b[:, 8:])
    return jnp.concatenate([v.reshape(MAIN, 128) for v in parts], axis=1)


def pack_tail(wire, g, rows):
    t = [quarter(rows, q).reshape(SIZE // 2, 8, 128) for q in range(4)]
    e01, o01 = swap(t[0], t[1])
    e23, o23 = swap(t[2], t[3])
    even = jnp.concatenate([e01, e23], axis=1)
    odd = jnp.concatenate([o01, o23], axis=1)
    both = jnp.stack([even, odd], axis=1).reshape(SIZE, 16, 128)
    wire[pl.ds(g * SIZE, SIZE), 32:48, :] = both.astype(BF)


def unpack_tail(wire, g):
    t = wire[pl.ds(g * SIZE, SIZE), 32:48, :].astype(F32).reshape(SIZE // 2, 2, 16, 128)
    even, odd = t[:, 0], t[:, 1]
    t0, t1 = swap(even[:, :8], odd[:, :8])
    t2, t3 = swap(even[:, 8:], odd[:, 8:])
    return jnp.concatenate([v.reshape(TAIL, 128) for v in (t0, t1, t2, t3)], axis=1)


def pack(wire, g, rows):
    pack_main(wire, g, rows[:MAIN])
    pack_tail(wire, g, rows[MAIN:])


def unpack(wire, g):
    return jnp.concatenate([unpack_main(wire, g), unpack_tail(wire, g)], axis=0)


def fold(rows):
    u = iota((LAST, 128), 0) & 7
    part = jnp.where(u == 2, quarter(rows, 2), quarter(rows, 3))
    return jnp.where(u == 0, quarter(rows, 0), jnp.where(u == 1, quarter(rows, 1), part))


def unfold(part):
    u = iota((LAST, 128), 0) & 7
    return jnp.concatenate([jnp.where(u == q, part, 0.0) for q in range(4)], axis=1)


def norm_forward(total):
    scale = lax.rsqrt(jnp.mean(total * total, axis=-1, keepdims=True) + 1e-05)
    return total * scale, scale


def norm_backward(grad, total, scale):
    inner = jnp.mean(grad * total, axis=-1, keepdims=True)
    return scale * (grad - total * (scale * scale * inner))


def gated(pre):
    gate = 0.5 * jnp.tanh(0.5 * pre) + 0.5
    value = pre * gate
    return value, gate + value * (1.0 - gate)


def kernel(*refs):
    inputs, refs = refs[:13], refs[13:]
    (out_ref, grid_grad, mesh_grad), refs = refs[:3], refs[3:]
    local, refs = refs[:13], refs[13:]
    grid_ref, mesh_ref, w_grid, w_recv, w_send, w_node, es, eo, et, ms, mo, mt, cot = local
    (
        send1, last1, recv1, rlast1, send2, recv2, back2, ret2, back1, blast1, ret1, tlast1,
        a1, a1t, a2, a2t, r1, r1t, r2, r2t, d1, d1l, d2,
        tm, rows1, gathered, total, hidden_ref,
        isem, ssem, rsem, lsem, zsem, ysem,
    ) = refs

    y, z, x, c = coords()
    gy = z * 8 + x * 2 + c

    loads = [pltpu.make_async_copy(a, b, isem.at[n]) for n, (a, b) in enumerate(zip(inputs, local))]
    order = (7, 10, 8, 11, 6, 9, 0, 2, 1, 3, 5, 4, 12)
    for n in order:
        loads[n].start()

    barrier = pltpu.get_barrier_semaphore()
    ring_x = [(y, z * 8 + ((x + d // 2) % 4) * 2 + (c + d) % 2) for d in range(1, 8)]
    ring_z = [(y, ((z + d) % 4) * 8 + x * 2 + c) for d in range(1, 4)]
    ring_y = [((y + d) % 4, gy) for d in range(1, 4)]

    def greet(sem, ring):
        for device in ring:
            pl.semaphore_signal(sem, inc=1, device_id=device, device_id_type=MESH)

    greet(barrier, ring_x + ring_z + ring_y)

    def route(owner):
        edges = owner.shape[1]
        dy = ((owner >> 5) - y) & 3
        dz = (((owner >> 3) & 3) - z) & 3
        dx = (((owner >> 1) & 3) - x) & 3
        dc = ((owner & 1) - c) & 1
        j = (((dy - dz - dx) & 3) * 2 + dc) * SIZE + dz * 4 + dx
        same = iota((PEERS, edges), 0) == j
        before = onehot(iota((edges, edges), 0) < iota((edges, edges), 1))
        count = mm(onehot(same), before)
        rank = jnp.sum(jnp.where(same, count, 0.0), axis=0, keepdims=True).astype(I32)
        return j, rank, onehot(same)

    def labels(rank, target, base):
        at = iota((128, rank.shape[1]), 0) == rank + base
        return jnp.where(at, (target + 1).astype(F32), 0.0).astype(BF)

    for n in (7, 10, 8, 11):
        loads[n].wait()
    j1, k1, same1 = route(eo[...])
    j2, k2, same2 = route(mo[...])
    tm[...] = (
        mm_nt(same1, labels(k1, et[...].reshape(1, -1), 0)) + mm_nt(same2, labels(k2, mt[...].reshape(1, -1), 16))
    ).astype(BF)

    pl.semaphore_wait(barrier, 13)
    greet(zsem, ring_z)

    loads[6].wait()
    edges1 = j1.shape[1]
    q1 = onehot(iota((grid_ref.shape[0], edges1), 0) == es[...].reshape(1, -1))
    main1 = jnp.where(k1 < 8, j1 * 8 + k1, -1)
    last1_of = jnp.where(k1 == 8, j1, -1)
    row1 = iota((MAIN, edges1), 0)
    for g in range(GROUPS):
        p_main = onehot(row1 + g * MAIN == main1)
        p_last = onehot(jnp.where((row1 & 7) < 4, (row1 >> 3) + g * SIZE, -2) == last1_of)
        p = jnp.concatenate([p_main, p_last], axis=0)
        a1[g] = mm_nt(p, q1).astype(BF)
        a1t[g] = mm_nt(q1, p).astype(BF)

    pl.semaphore_wait(zsem, 3)
    greet(ysem, ring_y)

    for n in (0, 2):
        loads[n].wait()
    rows1[...] = mm(grid_ref[...], w_grid[...]).astype(BF)
    for n in (1, 3):
        loads[n].wait()
    gathered[...] = mm(mesh_ref[...], w_recv[...]).astype(BF)

    pl.semaphore_wait(ysem, 3)

    def send_group(g, phase, wires, sign):
        gh, gl = g // 2, g % 2
        tc = (c + gl) % 2
        ty = [(y + sign * (gh + m) + 8) % 4 for m in range(4)]
        for k in range(SIZE):
            kz, kx = k // 4, k % 4
            tz, tx = (z + sign * kz + 4) % 4, (x + sign * kx + 4) % 4
            device = (ty[(kz + kx) % 4], tz * 8 + tx * 2 + tc)
            j = g * SIZE + k

            def remote():
                for src, dst, s, r in wires:
                    pltpu.make_async_remote_copy(
                        src.at[j], dst.at[j], s, r, device_id=device, device_id_type=MESH
                    ).start()

            def mine():
                for src, dst, s, r in wires:
                    pltpu.make_async_copy(src.at[j], dst.at[j], r).start()

            if k == 0:
                pl.when(g > 0)(remote)
                pl.when(g == 0)(mine)
            else:
                remote()

    def wait_group(g, dst, sem):
        at = dst.at[pl.ds(g * SIZE, SIZE)]
        pltpu.make_async_copy(at, at, sem).wait()

    mark = onehot(iota((LAST, SIZE), 0) == 8 * iota((LAST, SIZE), 1) + 4)
    unmark = onehot(iota((SIZE, LAST), 1) == 8 * iota((SIZE, LAST), 0) + 4)
    eye128 = onehot(iota((128, 128), 0) == iota((128, 128), 1))

    def slot_maps(rows):
        s = iota((1, rows), 1)
        if rows == ROWS1:
            peer = (s & (MAIN - 1)) >> 3
            rank = jnp.where(s < MAIN, s & 7, jnp.where((s & 7) < 4, 8, NEVER))
        else:
            peer = jnp.where(s < MAIN, s >> 3, (s - MAIN) >> 2)
            rank = jnp.where(s < MAIN, s & 7, 8 + (s & 3))
        spread = onehot(peer == iota((SIZE, rows), 0))
        eye = onehot(iota((rows, rows), 0) == iota((rows, rows), 1))
        return spread, rank, eye

    maps1 = slot_maps(ROWS1)
    maps2 = slot_maps(ROWS2)

    def receivers(mine_t, maps, base, g, r, rt):
        spread, rank, eye = maps
        lines = mm(mine_t, spread)
        lane = iota(lines.shape, 0)
        row = jnp.sum(jnp.where(lane == rank + base, lines, 0.0), axis=0, keepdims=True)
        flag = onehot(row.astype(I32) == lane + 1)
        rt[g] = flag
        r[g] = mm_nt(eye, flag).astype(BF)

    def send_enc(g, carry):
        rows = mm(a1[g], rows1[...])
        label = mm(mark, tm[pl.ds(pl.multiple_of(g * SIZE, SIZE), SIZE), :])
        pack_main(send1, g, rows[:MAIN])
        last = fold(rows[MAIN:]) + label
        last1[pl.ds(g * SIZE, SIZE)] = last.reshape(SIZE, 8, 128).astype(BF)
        send_group(
            g,
            0,
            ((last1, rlast1, lsem.at[0], lsem.at[2 + g]), (send1, recv1, ssem.at[0], rsem.at[0, g])),
            1,
        )
        return carry

    lax.fori_loop(0, GROUPS, send_enc, 0)

    for n in (9,):
        loads[n].wait()
    edges2 = j2.shape[1]
    q2 = onehot(iota((mesh_ref.shape[0], edges2), 0) == ms[...].reshape(1, -1))
    inside2 = jnp.where(k2 < 8, (j2 & 15) * 8 + k2, MAIN + (j2 & 15) * 4 + k2 - 8)
    place2 = (j2 >> 4) * ROWS2 + inside2
    for g in range(GROUPS):
        p = onehot(iota((ROWS2, edges2), 0) + g * ROWS2 == place2)
        a2[g] = mm_nt(p, q2).astype(BF)
        a2t[g] = mm_nt(q2, p).astype(BF)

    total[...] = jnp.zeros_like(total)

    def take_enc(g, carry):
        wait_group(g, rlast1, lsem.at[2 + g])
        last = rlast1[pl.ds(g * SIZE, SIZE)].astype(F32).reshape(LAST, 128)
        mine = mm(unmark, last.astype(BF)).astype(BF)
        mine_t = mm_nt(eye128, mine).astype(BF)
        receivers(mine_t, maps1, 0, g, r1, r1t)
        receivers(mine_t, maps2, 16, g, r2, r2t)
        picked = mm(r1[g], gathered[...])
        value_l, slope = gated(last + fold(picked[MAIN:]))
        d1l[g] = slope.astype(BF)
        wait_group(g, recv1, rsem.at[0, g])
        value, slope = gated(unpack_main(recv1, g) + picked[:MAIN])
        d1[g] = slope.astype(BF)
        both = jnp.concatenate([value.astype(BF), unfold(value_l).astype(BF)], axis=0)
        total[...] += mm(r1t[g], both)
        return carry

    lax.fori_loop(0, GROUPS, take_enc, 0)

    for n in (4, 5, 12):
        loads[n].wait()
    enc_sum = total[...]
    enc_norm, enc_scale = norm_forward(enc_sum)
    hidden = mesh_ref[...].astype(F32) + mm(enc_norm.astype(BF), w_node[...])
    hidden_ref[...] = hidden
    hidden_bf = hidden.astype(BF)
    rows1[pl.ds(0, 128), :] = mm(hidden_bf, w_send[...]).astype(BF)

    def send_msh(g, carry):
        pack(send2, g, mm(a2[g], rows1[pl.ds(0, 128), :]))
        send_group(g, 1, ((send2, recv2, ssem.at[1], rsem.at[1, g]),), 1)
        return carry

    lax.fori_loop(0, GROUPS, send_msh, 0)
    gathered[...] = mm(hidden_bf, w_recv[...]).astype(BF)
    cot_bf = cot[...]
    grad_norm = mm_nt(cot_bf, w_node[...]).astype(BF).astype(F32)
    total[...] = jnp.zeros_like(total)

    def take_msh(g, carry):
        picked = mm(r2[g], gathered[...])
        wait_group(g, recv2, rsem.at[1, g])
        value, slope = gated(unpack(recv2, g) + picked)
        d2[g] = slope.astype(BF)
        total[...] += mm(r2t[g], value.astype(BF))
        return carry

    lax.fori_loop(0, GROUPS, take_msh, 0)

    msh_sum = total[...]
    msh_norm, msh_scale = norm_forward(msh_sum)
    gathered[...] = norm_backward(grad_norm, msh_sum, msh_scale).astype(BF)

    def back_msh(g, carry):
        grad = mm(r2[g], gathered[...]) * d2[g].astype(F32)
        pack(back2, g, grad)
        send_group(g, 2, ((back2, ret2, ssem.at[2], rsem.at[2, g]),), -1)
        d2[g] = grad.astype(BF)
        return carry

    lax.fori_loop(0, GROUPS, back_msh, 0)
    out_ref[...] = (hidden_ref[...] + mm(msh_norm.astype(BF), w_node[...])).astype(BF)
    total[...] = jnp.zeros_like(total)

    def sum_msh(g, carry):
        total[...] += mm(r2t[g], d2[g])
        return carry

    lax.fori_loop(0, GROUPS, sum_msh, 0)
    part = mm_nt(total[...].astype(BF), w_recv[...])
    total[...] = jnp.zeros_like(total)

    def take_back_msh(g, carry):
        wait_group(g, ret2, rsem.at[2, g])
        total[...] += mm(a2t[g], unpack(ret2, g).astype(BF))
        return carry

    lax.fori_loop(0, GROUPS, take_back_msh, 0)
    grad_hidden_bf = (part + mm_nt(total[...].astype(BF), w_send[...])).astype(BF)
    grad_hidden = (cot_bf.astype(F32) + grad_hidden_bf.astype(F32)).astype(BF)
    grad_norm1 = mm_nt(grad_hidden, w_node[...]).astype(BF).astype(F32)
    gathered[...] = norm_backward(grad_norm1, enc_sum, enc_scale).astype(BF)

    def back_enc(g, carry):
        picked = mm(r1[g], gathered[...])
        grad = picked[:MAIN] * d1[g].astype(F32)
        grad_l = fold(picked[MAIN:]) * d1l[g].astype(F32)
        pack_main(back1, g, grad)
        blast1[pl.ds(g * SIZE, SIZE)] = grad_l.reshape(SIZE, 8, 128)[:, :4].astype(BF)
        send_group(
            g,
            3,
            ((blast1, tlast1, lsem.at[1], lsem.at[10 + g]), (back1, ret1, ssem.at[3], rsem.at[3, g])),
            -1,
        )
        d1[g] = grad.astype(BF)
        d1l[g] = grad_l.astype(BF)
        return carry

    lax.fori_loop(0, GROUPS, back_enc, 0)
    total[...] = jnp.zeros_like(total)

    def sum_enc(g, carry):
        both = jnp.concatenate([d1[g], unfold(d1l[g].astype(F32)).astype(BF)], axis=0)
        total[...] += mm(r1t[g], both)
        return carry

    lax.fori_loop(0, GROUPS, sum_enc, 0)
    mesh_part = mm_nt(total[...].astype(BF), w_recv[...]).astype(BF)
    mesh_grad[...] = (grad_hidden.astype(F32) + mesh_part.astype(F32)).astype(BF)

    def take_back_enc(g, carry):
        wait_group(g, tlast1, lsem.at[10 + g])
        half = tlast1[pl.ds(g * SIZE, SIZE)].astype(F32)
        last = jnp.concatenate([half, jnp.zeros_like(half)], axis=1).reshape(LAST, 128)
        wait_group(g, ret1, rsem.at[3, g])
        both = jnp.concatenate([unpack_main(ret1, g).astype(BF), unfold(last).astype(BF)], axis=0)
        return carry + mm(a1t[g], both)

    grid_rows = lax.fori_loop(0, GROUPS, take_back_enc, jnp.zeros(grid_ref.shape, F32))
    grid_grad[...] = mm_nt(grid_rows.astype(BF), w_grid[...]).astype(BF)

    for src, sem in (
        (send1, ssem.at[0]),
        (send2, ssem.at[1]),
        (back2, ssem.at[2]),
        (back1, ssem.at[3]),
        (last1, lsem.at[0]),
        (blast1, lsem.at[1]),
    ):
        at = src.at[pl.ds(1, PEERS - 1)]
        pltpu.make_async_copy(at, at, sem).wait()


def body(*args):
    grid_latent, mesh_latent = args[:2]
    args = [v.reshape(1, -1) if n in (7, 10) else v for n, v in enumerate(args)]
    vmem = pl.BlockSpec(memory_space=pltpu.VMEM)
    anywhere = pl.BlockSpec(memory_space=pl.ANY)
    nodes, width = mesh_latent.shape
    grid_nodes = grid_latent.shape[0]

    def block(*shape):
        return pltpu.VMEM(shape, BF)

    scratch = [pltpu.VMEM(v.shape, v.dtype) for v in args]
    scratch += [
        block(PEERS, 32, 128),
        block(PEERS, 8, 128),
        block(PEERS, 32, 128),
        block(PEERS, 8, 128),
        block(PEERS, 48, 128),
        block(PEERS, 48, 128),
        block(PEERS, 48, 128),
        block(PEERS, 48, 128),
        block(PEERS, 32, 128),
        block(PEERS, 4, 128),
        block(PEERS, 32, 128),
        block(PEERS, 4, 128),
        block(GROUPS, ROWS1, grid_nodes),
        block(GROUPS, grid_nodes, ROWS1),
        block(GROUPS, ROWS2, nodes),
        block(GROUPS, nodes, ROWS2),
        block(GROUPS, ROWS1, nodes),
        block(GROUPS, nodes, ROWS1),
        block(GROUPS, ROWS2, nodes),
        block(GROUPS, nodes, ROWS2),
        block(GROUPS, MAIN, width),
        block(GROUPS, LAST, 128),
        block(GROUPS, ROWS2, width),
        block(PEERS, 128),
        block(grid_nodes, width),
        block(nodes, width),
        pltpu.VMEM((nodes, width), F32),
        pltpu.VMEM((nodes, width), F32),
        pltpu.SemaphoreType.DMA((13,)),
        pltpu.SemaphoreType.DMA((4,)),
        pltpu.SemaphoreType.DMA((4, GROUPS)),
        pltpu.SemaphoreType.DMA((2 + 2 * GROUPS,)),
        pltpu.SemaphoreType.REGULAR,
        pltpu.SemaphoreType.REGULAR,
    ]
    return pl.pallas_call(
        kernel,
        out_shape=(
            jax.ShapeDtypeStruct(mesh_latent.shape, BF),
            jax.ShapeDtypeStruct(grid_latent.shape, BF),
            jax.ShapeDtypeStruct(mesh_latent.shape, BF),
        ),
        in_specs=[anywhere] * 13,
        out_specs=[vmem] * 3,
        scratch_shapes=scratch,
        compiler_params=pltpu.CompilerParams(
            collective_id=0, has_side_effects=True, vmem_limit_bytes=56 << 20
        ),
    )(*args)


def solution(mesh):
    rows = P(("gx", "gy"), None)
    flat = P(("gx", "gy"))
    placed = (rows, rows, P(), P(), P(), P(), flat, rows, flat, flat, rows, flat, rows)
    return jax.shard_map(
        body, mesh=mesh, in_specs=placed, out_specs=(rows, rows, rows), check_vma=False
    )
```

```python
import jax
import jax.numpy as jnp
from jax import lax
from jax.experimental import pallas as pl
from jax.experimental.pallas import tpu as pltpu
from jax.sharding import PartitionSpec as P

MESH = pl.DeviceIdType.MESH
BF = jnp.bfloat16
F32 = jnp.float32
I32 = jnp.int32

PEERS = 128
GROUPS = 8
SIZE = 16
MAIN = SIZE * 8
TAIL = SIZE * 4
LAST = SIZE * 8
ROWS1 = MAIN + LAST
ROWS2 = MAIN + TAIL
NEVER = 99
NEAR_LAST = sorted(range(SIZE), key=lambda k: -min(k // 4, 4 - k // 4) - min(k % 4, 4 - k % 4))


def coords():
    y = lax.axis_index("gx")
    g = lax.axis_index("gy")
    return y, g // 8, (g // 2) % 4, g % 2


def iota(shape, axis):
    return lax.broadcasted_iota(I32, shape, axis)


def onehot(mask):
    return jnp.where(mask, 1.0, 0.0).astype(BF)


def mm(a, b):
    return lax.dot_general(a, b, (((1,), (0,)), ((), ())), preferred_element_type=F32)


def mm_nt(a, b):
    return lax.dot_general(a, b, (((1,), (1,)), ((), ())), preferred_element_type=F32)


def quarter(v, q):
    return v[..., q * 128 : q * 128 + 128]


def swap(a, b):
    low = iota(a.shape, 1) < 4
    return jnp.where(low, a, pltpu.roll(b, 4, 1)), jnp.where(low, pltpu.roll(a, 4, 1), b)


def pack_main(wire, g, rows):
    at = pl.ds(g * SIZE, SIZE)
    m = [quarter(rows, q).reshape(SIZE, 8, 128) for q in range(4)]
    wire[at, 0:16, :] = jnp.concatenate([m[0], m[1]], axis=1).astype(BF)
    wire[at, 16:32, :] = jnp.concatenate([m[2], m[3]], axis=1).astype(BF)


def unpack_main(wire, g):
    at = pl.ds(g * SIZE, SIZE)
    a = wire[at, 0:16, :].astype(F32)
    b = wire[at, 16:32, :].astype(F32)
    parts = (a[:, :8], a[:, 8:], b[:, :8], b[:, 8:])
    return jnp.concatenate([v.reshape(MAIN, 128) for v in parts], axis=1)


def pack_units(wire, g, rows, last):
    at = pl.ds(g * SIZE, SIZE)
    for q in range(4):
        m = quarter(rows, q).reshape(SIZE, 8, 128)
        wire[at, 2 * q] = m[:, :4].astype(BF)
        wire[at, 2 * q + 1] = m[:, 4:].astype(BF)
    last = last.reshape(SIZE, 8, 128)
    wire[at, 8] = last[:, :4].astype(BF)
    if wire.shape[1] > 9:
        wire[at, 9] = last[:, 4:].astype(BF)


def unpack_units(wire, g):
    at = pl.ds(g * SIZE, SIZE)

    def pair(n):
        low = wire[at, n].astype(F32)
        high = wire[at, n + 1].astype(F32) if n + 1 < wire.shape[1] else jnp.zeros_like(low)
        return jnp.concatenate([low, high], axis=1).reshape(MAIN, 128)

    return jnp.concatenate([pair(2 * q) for q in range(4)], axis=1), pair(8)


def pack_tail(wire, g, rows):
    t = [quarter(rows, q).reshape(SIZE // 2, 8, 128) for q in range(4)]
    e01, o01 = swap(t[0], t[1])
    e23, o23 = swap(t[2], t[3])
    even = jnp.concatenate([e01, e23], axis=1)
    odd = jnp.concatenate([o01, o23], axis=1)
    both = jnp.stack([even, odd], axis=1).reshape(SIZE, 16, 128)
    wire[pl.ds(g * SIZE, SIZE), 32:48, :] = both.astype(BF)


def unpack_tail(wire, g):
    t = wire[pl.ds(g * SIZE, SIZE), 32:48, :].astype(F32).reshape(SIZE // 2, 2, 16, 128)
    even, odd = t[:, 0], t[:, 1]
    t0, t1 = swap(even[:, :8], odd[:, :8])
    t2, t3 = swap(even[:, 8:], odd[:, 8:])
    return jnp.concatenate([v.reshape(TAIL, 128) for v in (t0, t1, t2, t3)], axis=1)


def pack(wire, g, rows):
    pack_main(wire, g, rows[:MAIN])
    pack_tail(wire, g, rows[MAIN:])


def unpack(wire, g):
    return jnp.concatenate([unpack_main(wire, g), unpack_tail(wire, g)], axis=0)


def fold(rows):
    u = iota((LAST, 128), 0) & 7
    part = jnp.where(u == 2, quarter(rows, 2), quarter(rows, 3))
    return jnp.where(u == 0, quarter(rows, 0), jnp.where(u == 1, quarter(rows, 1), part))


def unfold(part):
    u = iota((LAST, 128), 0) & 7
    return jnp.concatenate([jnp.where(u == q, part, 0.0) for q in range(4)], axis=1)


def norm_forward(total):
    scale = lax.rsqrt(jnp.mean(total * total, axis=-1, keepdims=True) + 1e-05)
    return total * scale, scale


def norm_backward(grad, total, scale):
    inner = jnp.mean(grad * total, axis=-1, keepdims=True)
    return scale * (grad - total * (scale * scale * inner))


def gated(pre):
    gate = 0.5 * jnp.tanh(0.5 * pre) + 0.5
    value = pre * gate
    return value, gate + value * (1.0 - gate)


def kernel(*refs):
    inputs, refs = refs[:13], refs[13:]
    (out_ref, grid_grad, mesh_grad), refs = refs[:3], refs[3:]
    local, refs = refs[:13], refs[13:]
    grid_ref, mesh_ref, w_grid, w_recv, w_send, w_node, es, eo, et, ms, mo, mt, cot = local
    (
        send1, recv1, send2, recv2, back2, ret2, back1, ret1,
        a1, a1t, a2, a2t, r1, r1t, r2, r2t, d1, d1l, d2,
        tm, rows1, gathered, total, hidden_ref,
        isem, ssem, rsem, psem,
    ) = refs

    y, z, x, c = coords()

    loads = [pltpu.make_async_copy(a, b, isem.at[n]) for n, (a, b) in enumerate(zip(inputs, local))]
    order = (7, 10, 8, 11, 6, 9, 0, 2, 1, 3, 5, 4, 12)
    for n in order:
        loads[n].start()

    barrier = pltpu.get_barrier_semaphore()
    ring = [(y, z * 8 + ((x + d // 2) % 4) * 2 + (c + d) % 2) for d in range(1, 8)]
    plane = [((y + d // 4) % 4, ((z + d) % 4) * 8 + x * 2 + c) for d in range(1, 16)]

    def greet(sem, ring):
        for device in ring:
            pl.semaphore_signal(sem, inc=1, device_id=device, device_id_type=MESH)

    greet(barrier, ring + plane)

    def route(owner):
        edges = owner.shape[1]
        dy = ((owner >> 5) - y) & 3
        dz = (((owner >> 3) & 3) - z) & 3
        dx = (((owner >> 1) & 3) - x) & 3
        dc = ((owner & 1) - c) & 1
        j = (((dy - dz - dx) & 3) * 2 + dc) * SIZE + dz * 4 + dx
        same = iota((PEERS, edges), 0) == j
        before = onehot(iota((edges, edges), 0) < iota((edges, edges), 1))
        count = mm(onehot(same), before)
        rank = jnp.sum(jnp.where(same, count, 0.0), axis=0, keepdims=True).astype(I32)
        return j, rank, onehot(same)

    def labels(rank, target, base):
        at = iota((128, rank.shape[1]), 0) == rank + base
        return jnp.where(at, (target + 1).astype(F32), 0.0).astype(BF)

    for n in (7, 10, 8, 11):
        loads[n].wait()
    j1, k1, same1 = route(eo[...])
    j2, k2, same2 = route(mo[...])
    tm[...] = (
        mm_nt(same1, labels(k1, et[...].reshape(1, -1), 0)) + mm_nt(same2, labels(k2, mt[...].reshape(1, -1), 16))
    ).astype(BF)

    pl.semaphore_wait(barrier, 22)
    greet(psem, plane)

    loads[6].wait()
    edges1 = j1.shape[1]
    q1 = onehot(iota((grid_ref.shape[0], edges1), 0) == es[...].reshape(1, -1))
    main1 = jnp.where(k1 < 8, j1 * 8 + k1, -1)
    last1_of = jnp.where(k1 == 8, j1, -1)
    row1 = iota((MAIN, edges1), 0)
    for g in range(GROUPS):
        p_main = onehot(row1 + g * MAIN == main1)
        p_last = onehot(jnp.where((row1 & 7) < 4, (row1 >> 3) + g * SIZE, -2) == last1_of)
        p = jnp.concatenate([p_main, p_last], axis=0)
        a1[g] = mm_nt(p, q1).astype(BF)
        a1t[g] = mm_nt(q1, p).astype(BF)

    for n in (0, 2):
        loads[n].wait()
    rows1[...] = mm(grid_ref[...], w_grid[...]).astype(BF)
    for n in (1, 3):
        loads[n].wait()
    gathered[...] = mm(mesh_ref[...], w_recv[...]).astype(BF)

    pl.semaphore_wait(psem, 15)

    def send_group(g, src, dst, s, r, sign):
        gh, gl = g // 2, g % 2
        tc = (c + gl) % 2
        ty = [(y + sign * (gh + m) + 8) % 4 for m in range(4)]
        for k in NEAR_LAST:
            kz, kx = k // 4, k % 4
            tz, tx = (z + sign * kz + 4) % 4, (x + sign * kx + 4) % 4
            device = (ty[(kz + kx) % 4], tz * 8 + tx * 2 + tc)
            j = g * SIZE + k

            def remote():
                pltpu.make_async_remote_copy(
                    src.at[j], dst.at[j], s, r, device_id=device, device_id_type=MESH
                ).start()

            def mine():
                pltpu.make_async_copy(src.at[j], dst.at[j], r).start()

            if k == 0:
                pl.when(g > 0)(remote)
                pl.when(g == 0)(mine)
            else:
                remote()

    def wait_group(g, dst, sem):
        at = dst.at[pl.ds(g * SIZE, SIZE)]
        pltpu.make_async_copy(at, at, sem).wait()

    mark = onehot(iota((LAST, SIZE), 0) == 8 * iota((LAST, SIZE), 1) + 4)
    unmark = onehot(iota((SIZE, LAST), 1) == 8 * iota((SIZE, LAST), 0) + 4)
    eye128 = onehot(iota((128, 128), 0) == iota((128, 128), 1))

    def slot_maps(rows):
        s = iota((1, rows), 1)
        if rows == ROWS1:
            peer = (s & (MAIN - 1)) >> 3
            rank = jnp.where(s < MAIN, s & 7, jnp.where((s & 7) < 4, 8, NEVER))
        else:
            peer = jnp.where(s < MAIN, s >> 3, (s - MAIN) >> 2)
            rank = jnp.where(s < MAIN, s & 7, 8 + (s & 3))
        spread = onehot(peer == iota((SIZE, rows), 0))
        eye = onehot(iota((rows, rows), 0) == iota((rows, rows), 1))
        return spread, rank, eye

    maps1 = slot_maps(ROWS1)
    maps2 = slot_maps(ROWS2)

    def receivers(mine_t, maps, base, g, r, rt):
        spread, rank, eye = maps
        lines = mm(mine_t, spread)
        lane = iota(lines.shape, 0)
        row = jnp.sum(jnp.where(lane == rank + base, lines, 0.0), axis=0, keepdims=True)
        flag = onehot(row.astype(I32) == lane + 1)
        rt[g] = flag
        r[g] = mm_nt(eye, flag).astype(BF)

    def send_enc(g, carry):
        rows = mm(a1[g], rows1[...])
        label = mm(mark, tm[pl.ds(pl.multiple_of(g * SIZE, SIZE), SIZE), :])
        pack_units(send1, g, rows[:MAIN], fold(rows[MAIN:]) + label)
        send_group(g, send1, recv1, ssem.at[0], rsem.at[0, g], 1)
        return carry

    lax.fori_loop(0, GROUPS, send_enc, 0)

    for n in (9,):
        loads[n].wait()
    edges2 = j2.shape[1]
    q2 = onehot(iota((mesh_ref.shape[0], edges2), 0) == ms[...].reshape(1, -1))
    inside2 = jnp.where(k2 < 8, (j2 & 15) * 8 + k2, MAIN + (j2 & 15) * 4 + k2 - 8)
    place2 = (j2 >> 4) * ROWS2 + inside2
    for g in range(GROUPS):
        p = onehot(iota((ROWS2, edges2), 0) + g * ROWS2 == place2)
        a2[g] = mm_nt(p, q2).astype(BF)
        a2t[g] = mm_nt(q2, p).astype(BF)

    total[...] = jnp.zeros_like(total)

    def take_enc(g, carry):
        wait_group(g, recv1, rsem.at[0, g])
        rows, last = unpack_units(recv1, g)
        mine = mm(unmark, last.astype(BF)).astype(BF)
        mine_t = mm_nt(eye128, mine).astype(BF)
        receivers(mine_t, maps1, 0, g, r1, r1t)
        receivers(mine_t, maps2, 16, g, r2, r2t)
        picked = mm(r1[g], gathered[...])
        value_l, slope = gated(last + fold(picked[MAIN:]))
        d1l[g] = slope.astype(BF)
        value, slope = gated(rows + picked[:MAIN])
        d1[g] = slope.astype(BF)
        both = jnp.concatenate([value.astype(BF), unfold(value_l).astype(BF)], axis=0)
        total[...] += mm(r1t[g], both)
        return carry

    lax.fori_loop(0, GROUPS, take_enc, 0)

    for n in (4, 5, 12):
        loads[n].wait()
    enc_sum = total[...]
    enc_norm, enc_scale = norm_forward(enc_sum)
    hidden = mesh_ref[...].astype(F32) + mm(enc_norm.astype(BF), w_node[...])
    hidden_ref[...] = hidden
    hidden_bf = hidden.astype(BF)
    rows1[pl.ds(0, 128), :] = mm(hidden_bf, w_send[...]).astype(BF)

    def send_msh(g, carry):
        pack(send2, g, mm(a2[g], rows1[pl.ds(0, 128), :]))
        send_group(g, send2, recv2, ssem.at[1], rsem.at[1, g], 1)
        return carry

    lax.fori_loop(0, GROUPS, send_msh, 0)
    gathered[...] = mm(hidden_bf, w_recv[...]).astype(BF)
    cot_bf = cot[...]
    grad_norm = mm_nt(cot_bf, w_node[...]).astype(BF).astype(F32)
    total[...] = jnp.zeros_like(total)

    def take_msh(g, carry):
        picked = mm(r2[g], gathered[...])
        wait_group(g, recv2, rsem.at[1, g])
        value, slope = gated(unpack(recv2, g) + picked)
        d2[g] = slope.astype(BF)
        total[...] += mm(r2t[g], value.astype(BF))
        return carry

    lax.fori_loop(0, GROUPS, take_msh, 0)

    msh_sum = total[...]
    msh_norm, msh_scale = norm_forward(msh_sum)
    gathered[...] = norm_backward(grad_norm, msh_sum, msh_scale).astype(BF)

    def back_msh(g, carry):
        grad = mm(r2[g], gathered[...]) * d2[g].astype(F32)
        pack(back2, g, grad)
        send_group(g, back2, ret2, ssem.at[2], rsem.at[2, g], -1)
        d2[g] = grad.astype(BF)
        return carry

    lax.fori_loop(0, GROUPS, back_msh, 0)
    out_ref[...] = (hidden_ref[...] + mm(msh_norm.astype(BF), w_node[...])).astype(BF)
    total[...] = jnp.zeros_like(total)

    def sum_msh(g, carry):
        total[...] += mm(r2t[g], d2[g])
        return carry

    lax.fori_loop(0, GROUPS, sum_msh, 0)
    part = mm_nt(total[...].astype(BF), w_recv[...])
    total[...] = jnp.zeros_like(total)

    def take_back_msh(g, carry):
        wait_group(g, ret2, rsem.at[2, g])
        total[...] += mm(a2t[g], unpack(ret2, g).astype(BF))
        return carry

    lax.fori_loop(0, GROUPS, take_back_msh, 0)
    grad_hidden_bf = (part + mm_nt(total[...].astype(BF), w_send[...])).astype(BF)
    grad_hidden = (cot_bf.astype(F32) + grad_hidden_bf.astype(F32)).astype(BF)
    grad_norm1 = mm_nt(grad_hidden, w_node[...]).astype(BF).astype(F32)
    gathered[...] = norm_backward(grad_norm1, enc_sum, enc_scale).astype(BF)

    def back_enc(g, carry):
        picked = mm(r1[g], gathered[...])
        grad = picked[:MAIN] * d1[g].astype(F32)
        grad_l = fold(picked[MAIN:]) * d1l[g].astype(F32)
        pack_units(back1, g, grad, grad_l)
        send_group(g, back1, ret1, ssem.at[3], rsem.at[3, g], -1)
        d1[g] = grad.astype(BF)
        d1l[g] = grad_l.astype(BF)
        return carry

    lax.fori_loop(0, GROUPS, back_enc, 0)
    total[...] = jnp.zeros_like(total)

    def sum_enc(g, carry):
        both = jnp.concatenate([d1[g], unfold(d1l[g].astype(F32)).astype(BF)], axis=0)
        total[...] += mm(r1t[g], both)
        return carry

    lax.fori_loop(0, GROUPS, sum_enc, 0)
    mesh_part = mm_nt(total[...].astype(BF), w_recv[...]).astype(BF)
    mesh_grad[...] = (grad_hidden.astype(F32) + mesh_part.astype(F32)).astype(BF)

    def take_back_enc(g, carry):
        wait_group(g, ret1, rsem.at[3, g])
        rows, last = unpack_units(ret1, g)
        both = jnp.concatenate([rows.astype(BF), unfold(last).astype(BF)], axis=0)
        return carry + mm(a1t[g], both)

    grid_rows = lax.fori_loop(0, GROUPS, take_back_enc, jnp.zeros(grid_ref.shape, F32))
    grid_grad[...] = mm_nt(grid_rows.astype(BF), w_grid[...]).astype(BF)

    for src, sem in (
        (send1, ssem.at[0]),
        (send2, ssem.at[1]),
        (back2, ssem.at[2]),
        (back1, ssem.at[3]),
    ):
        at = src.at[pl.ds(1, PEERS - 1)]
        pltpu.make_async_copy(at, at, sem).wait()


def hand_on(*refs):
    for n in range(3):
        refs[n + 3][...] = refs[n][...]


def body(*args):
    grid_latent, mesh_latent = args[:2]
    args = [v.reshape(1, -1) if n in (7, 10) else v for n, v in enumerate(args)]
    vmem = pl.BlockSpec(memory_space=pltpu.VMEM)
    anywhere = pl.BlockSpec(memory_space=pl.ANY)
    nodes, width = mesh_latent.shape
    grid_nodes = grid_latent.shape[0]

    def block(*shape):
        return pltpu.VMEM(shape, BF)

    scratch = [pltpu.VMEM(v.shape, v.dtype) for v in args]
    scratch += [
        block(PEERS, 10, 4, 128),
        block(PEERS, 10, 4, 128),
        block(PEERS, 48, 128),
        block(PEERS, 48, 128),
        block(PEERS, 48, 128),
        block(PEERS, 48, 128),
        block(PEERS, 9, 4, 128),
        block(PEERS, 9, 4, 128),
        block(GROUPS, ROWS1, grid_nodes),
        block(GROUPS, grid_nodes, ROWS1),
        block(GROUPS, ROWS2, nodes),
        block(GROUPS, nodes, ROWS2),
        block(GROUPS, ROWS1, nodes),
        block(GROUPS, nodes, ROWS1),
        block(GROUPS, ROWS2, nodes),
        block(GROUPS, nodes, ROWS2),
        block(GROUPS, MAIN, width),
        block(GROUPS, LAST, 128),
        block(GROUPS, ROWS2, width),
        block(PEERS, 128),
        block(grid_nodes, width),
        block(nodes, width),
        pltpu.VMEM((nodes, width), F32),
        pltpu.VMEM((nodes, width), F32),
        pltpu.SemaphoreType.DMA((13,)),
        pltpu.SemaphoreType.DMA((4,)),
        pltpu.SemaphoreType.DMA((4, GROUPS)),
        pltpu.SemaphoreType.REGULAR,
    ]
    results = pl.pallas_call(
        kernel,
        out_shape=(
            jax.ShapeDtypeStruct(mesh_latent.shape, BF),
            jax.ShapeDtypeStruct(grid_latent.shape, BF),
            jax.ShapeDtypeStruct(mesh_latent.shape, BF),
        ),
        in_specs=[anywhere] * 13,
        out_specs=[vmem] * 3,
        scratch_shapes=scratch,
        compiler_params=pltpu.CompilerParams(
            collective_id=0, has_side_effects=True, vmem_limit_bytes=56 << 20
        ),
    )(*args)
    return pl.pallas_call(
        hand_on,
        out_shape=[jax.ShapeDtypeStruct(v.shape, v.dtype) for v in results],
        in_specs=[vmem] * 3,
        out_specs=[vmem] * 3,
    )(*results)


def solution(mesh):
    rows = P(("gx", "gy"), None)
    flat = P(("gx", "gy"))
    placed = (rows, rows, P(), P(), P(), P(), flat, rows, flat, flat, rows, flat, rows)
    return jax.shard_map(
        body, mesh=mesh, in_specs=placed, out_specs=(rows, rows, rows), check_vma=False
    )
```

```python
import jax
import jax.numpy as jnp
from jax import lax
from jax.experimental import pallas as pl
from jax.experimental.pallas import tpu as pltpu
from jax.sharding import PartitionSpec as P

MESH = pl.DeviceIdType.MESH
BF = jnp.bfloat16
F32 = jnp.float32
I32 = jnp.int32

PEERS = 128
GROUPS = 8
SIZE = 16
MAIN = SIZE * 8
TAIL = SIZE * 4
LAST = SIZE * 8
ROWS1 = MAIN + LAST
ROWS2 = MAIN + TAIL
NEVER = 99
NEAR_LAST = sorted(range(SIZE), key=lambda k: -min(k // 4, 4 - k // 4) - min(k % 4, 4 - k % 4))


def coords():
    y = lax.axis_index("gx")
    g = lax.axis_index("gy")
    return y, g // 8, (g // 2) % 4, g % 2


def iota(shape, axis):
    return lax.broadcasted_iota(I32, shape, axis)


def onehot(mask):
    return jnp.where(mask, 1.0, 0.0).astype(BF)


def mm(a, b):
    return lax.dot_general(a, b, (((1,), (0,)), ((), ())), preferred_element_type=F32)


def mm_nt(a, b):
    return lax.dot_general(a, b, (((1,), (1,)), ((), ())), preferred_element_type=F32)


def quarter(v, q):
    return v[..., q * 128 : q * 128 + 128]


def swap(a, b):
    low = iota(a.shape, 1) < 4
    return jnp.where(low, a, pltpu.roll(b, 4, 1)), jnp.where(low, pltpu.roll(a, 4, 1), b)


def pack_main(wire, g, rows):
    at = pl.ds(g * SIZE, SIZE)
    m = [quarter(rows, q).reshape(SIZE, 8, 128) for q in range(4)]
    wire[at, 0:16, :] = jnp.concatenate([m[0], m[1]], axis=1).astype(BF)
    wire[at, 16:32, :] = jnp.concatenate([m[2], m[3]], axis=1).astype(BF)


def unpack_main(wire, g):
    at = pl.ds(g * SIZE, SIZE)
    a = wire[at, 0:16, :].astype(F32)
    b = wire[at, 16:32, :].astype(F32)
    parts = (a[:, :8], a[:, 8:], b[:, :8], b[:, 8:])
    return jnp.concatenate([v.reshape(MAIN, 128) for v in parts], axis=1)


def pack_units(wire, g, rows, last):
    at = pl.ds(g * SIZE, SIZE)
    for q in range(4):
        m = quarter(rows, q).reshape(SIZE, 8, 128)
        wire[at, 2 * q] = m[:, :4].astype(BF)
        wire[at, 2 * q + 1] = m[:, 4:].astype(BF)
    last = last.reshape(SIZE, 8, 128)
    wire[at, 8] = last[:, :4].astype(BF)


def unpack_units(wire, g):
    at = pl.ds(g * SIZE, SIZE)

    def pair(n):
        low = wire[at, n].astype(F32)
        high = wire[at, n + 1].astype(F32) if n + 1 < wire.shape[1] else jnp.zeros_like(low)
        return jnp.concatenate([low, high], axis=1).reshape(MAIN, 128)

    return jnp.concatenate([pair(2 * q) for q in range(4)], axis=1), pair(8)


def pack_tail(wire, g, rows):
    t = [quarter(rows, q).reshape(SIZE // 2, 8, 128) for q in range(4)]
    e01, o01 = swap(t[0], t[1])
    e23, o23 = swap(t[2], t[3])
    even = jnp.concatenate([e01, e23], axis=1)
    odd = jnp.concatenate([o01, o23], axis=1)
    both = jnp.stack([even, odd], axis=1).reshape(SIZE, 16, 128)
    wire[pl.ds(g * SIZE, SIZE), 32:48, :] = both.astype(BF)


def unpack_tail(wire, g):
    t = wire[pl.ds(g * SIZE, SIZE), 32:48, :].astype(F32).reshape(SIZE // 2, 2, 16, 128)
    even, odd = t[:, 0], t[:, 1]
    t0, t1 = swap(even[:, :8], odd[:, :8])
    t2, t3 = swap(even[:, 8:], odd[:, 8:])
    return jnp.concatenate([v.reshape(TAIL, 128) for v in (t0, t1, t2, t3)], axis=1)


def pack(wire, g, rows):
    pack_main(wire, g, rows[:MAIN])
    pack_tail(wire, g, rows[MAIN:])


def unpack(wire, g):
    return jnp.concatenate([unpack_main(wire, g), unpack_tail(wire, g)], axis=0)


def fold(rows):
    u = iota((LAST, 128), 0) & 7
    part = jnp.where(u == 2, quarter(rows, 2), quarter(rows, 3))
    return jnp.where(u == 0, quarter(rows, 0), jnp.where(u == 1, quarter(rows, 1), part))


def unfold(part):
    u = iota((LAST, 128), 0) & 7
    return jnp.concatenate([jnp.where(u == q, part, 0.0) for q in range(4)], axis=1)


def norm_forward(total):
    scale = lax.rsqrt(jnp.mean(total * total, axis=-1, keepdims=True) + 1e-05)
    return total * scale, scale


def norm_backward(grad, total, scale):
    inner = jnp.mean(grad * total, axis=-1, keepdims=True)
    return scale * (grad - total * (scale * scale * inner))


def gated(pre):
    gate = 0.5 * jnp.tanh(0.5 * pre) + 0.5
    value = pre * gate
    return value, gate + value * (1.0 - gate)


def kernel(*refs):
    inputs, refs = refs[:13], refs[13:]
    (out_ref, grid_grad, mesh_grad), refs = refs[:3], refs[3:]
    local, refs = refs[:13], refs[13:]
    grid_ref, mesh_ref, w_grid, w_recv, w_send, w_node, es, eo, et, ms, mo, mt, cot = local
    (
        send1, recv1, send2, recv2, back2, ret2, back1, ret1,
        a1, a1t, a2, a2t, r1, r1t, r2, r2t, d1, d1l, d2,
        told, ring_told, plane_told, heard, rows1, gathered, total, hidden_ref,
        isem, ssem, rsem, rlsem, plsem, psem,
    ) = refs

    y, z, x, c = coords()

    loads = [pltpu.make_async_copy(a, b, isem.at[n]) for n, (a, b) in enumerate(zip(inputs, local))]
    order = (7, 10, 8, 11, 6, 9, 0, 2, 1, 3, 5, 4, 12)
    for n in order:
        loads[n].start()

    barrier = pltpu.get_barrier_semaphore()
    ring = [(y, z * 8 + ((x + d // 2) % 4) * 2 + (c + d) % 2) for d in range(1, 8)]
    plane = [((y + d // 4) % 4, ((z + d) % 4) * 8 + x * 2 + c) for d in range(1, 16)]

    def greet(sem, ring):
        for device in ring:
            pl.semaphore_signal(sem, inc=1, device_id=device, device_id_type=MESH)

    greet(barrier, ring + plane)

    def route(owner):
        edges = owner.shape[1]
        dy = ((owner >> 5) - y) & 3
        dz = (((owner >> 3) & 3) - z) & 3
        dx = (((owner >> 1) & 3) - x) & 3
        dc = ((owner & 1) - c) & 1
        j = (((dy - dz - dx) & 3) * 2 + dc) * SIZE + dz * 4 + dx
        same = iota((PEERS, edges), 0) == (dx * 2 + dc) * 16 + dy * 4 + dz
        before = onehot(iota((edges, edges), 0) < iota((edges, edges), 1))
        count = mm(onehot(same), before)
        rank = jnp.sum(jnp.where(same, count, 0.0), axis=0, keepdims=True).astype(I32)
        return j, rank, onehot(same)

    def labels(rank, target, base):
        at = iota((128, rank.shape[1]), 0) == rank + base
        return jnp.where(at, (target + 1).astype(F32), 0.0).astype(BF)

    for n in (7, 10, 8, 11):
        loads[n].wait()
    j1, k1, same1 = route(eo[...])
    j2, k2, same2 = route(mo[...])
    told[...] = (
        mm_nt(same1, labels(k1, et[...].reshape(1, -1), 0)) + mm_nt(same2, labels(k2, mt[...].reshape(1, -1), 16))
    ).astype(BF).reshape(8, 16, 128)

    pl.semaphore_wait(barrier, 22)
    greet(psem, plane)

    def pass_on(src, dst, sem, devices):
        pltpu.make_async_copy(src.at[0], dst.at[0], sem.at[1]).start()
        for n, device in enumerate(devices):
            pltpu.make_async_remote_copy(
                src.at[n + 1], dst.at[n + 1], sem.at[0], sem.at[1], device_id=device, device_id_type=MESH
            ).start()

    pass_on(told, ring_told, rlsem, ring)

    loads[6].wait()
    edges1 = j1.shape[1]
    q1 = onehot(iota((grid_ref.shape[0], edges1), 0) == es[...].reshape(1, -1))
    main1 = jnp.where(k1 < 8, j1 * 8 + k1, -1)
    last1_of = jnp.where(k1 == 8, j1, -1)
    row1 = iota((MAIN, edges1), 0)
    for g in range(GROUPS):
        p_main = onehot(row1 + g * MAIN == main1)
        p_last = onehot(jnp.where((row1 & 7) < 4, (row1 >> 3) + g * SIZE, -2) == last1_of)
        p = jnp.concatenate([p_main, p_last], axis=0)
        a1[g] = mm_nt(p, q1).astype(BF)
        a1t[g] = mm_nt(q1, p).astype(BF)

    for n in (0, 2):
        loads[n].wait()
    rows1[...] = mm(grid_ref[...], w_grid[...]).astype(BF)
    for n in (1, 3):
        loads[n].wait()
    gathered[...] = mm(mesh_ref[...], w_recv[...]).astype(BF)

    pl.semaphore_wait(psem, 15)

    def send_group(g, src, dst, s, r, sign):
        gh, gl = g // 2, g % 2
        tc = (c + gl) % 2
        ty = [(y + sign * (gh + m) + 8) % 4 for m in range(4)]
        for k in NEAR_LAST:
            kz, kx = k // 4, k % 4
            tz, tx = (z + sign * kz + 4) % 4, (x + sign * kx + 4) % 4
            device = (ty[(kz + kx) % 4], tz * 8 + tx * 2 + tc)
            j = g * SIZE + k

            def remote():
                pltpu.make_async_remote_copy(
                    src.at[j], dst.at[j], s, r, device_id=device, device_id_type=MESH
                ).start()

            def mine():
                pltpu.make_async_copy(src.at[j], dst.at[j], r).start()

            if k == 0:
                pl.when(g > 0)(remote)
                pl.when(g == 0)(mine)
            else:
                remote()

    def wait_group(g, dst, sem):
        at = dst.at[pl.ds(g * SIZE, SIZE)]
        pltpu.make_async_copy(at, at, sem).wait()

    eye128 = onehot(iota((128, 128), 0) == iota((128, 128), 1))

    def slot_maps(rows):
        s = iota((1, rows), 1)
        if rows == ROWS1:
            peer = (s & (MAIN - 1)) >> 3
            rank = jnp.where(s < MAIN, s & 7, jnp.where((s & 7) < 4, 8, NEVER))
        else:
            peer = jnp.where(s < MAIN, s >> 3, (s - MAIN) >> 2)
            rank = jnp.where(s < MAIN, s & 7, 8 + (s & 3))
        eye = onehot(iota((rows, rows), 0) == iota((rows, rows), 1))
        return peer, rank, eye

    maps1 = slot_maps(ROWS1)
    maps2 = slot_maps(ROWS2)

    def receivers(mine_t, maps, base, g, r, rt):
        peer, rank, eye = maps
        lines = mm(mine_t, onehot(iota((PEERS, rank.shape[1]), 0) == peer + g * SIZE))
        lane = iota(lines.shape, 0)
        row = jnp.sum(jnp.where(lane == rank + base, lines, 0.0), axis=0, keepdims=True)
        flag = onehot(row.astype(I32) == lane + 1)
        rt[g] = flag
        r[g] = mm_nt(eye, flag).astype(BF)

    def send_enc(g, carry):
        rows = mm(a1[g], rows1[...])
        pack_units(send1, g, rows[:MAIN], fold(rows[MAIN:]))
        send_group(g, send1, recv1, ssem.at[0], rsem.at[0, g], 1)
        return carry

    send_enc(0, 0)

    pltpu.make_async_copy(ring_told, ring_told, rlsem.at[1]).wait()
    line = iota((PEERS, PEERS), 0)
    turn = onehot(iota((PEERS, PEERS), 1) == (line & 7) * 16 + (line >> 3))
    plane_told[...] = mm(turn, ring_told[...].reshape(PEERS, 128)).reshape(16, 8, 128).astype(BF)
    pass_on(plane_told, heard, plsem, plane)

    lax.fori_loop(1, GROUPS, send_enc, 0)

    for n in (9,):
        loads[n].wait()
    edges2 = j2.shape[1]
    q2 = onehot(iota((mesh_ref.shape[0], edges2), 0) == ms[...].reshape(1, -1))
    inside2 = jnp.where(k2 < 8, (j2 & 15) * 8 + k2, MAIN + (j2 & 15) * 4 + k2 - 8)
    place2 = (j2 >> 4) * ROWS2 + inside2
    for g in range(GROUPS):
        p = onehot(iota((ROWS2, edges2), 0) + g * ROWS2 == place2)
        a2[g] = mm_nt(p, q2).astype(BF)
        a2t[g] = mm_nt(q2, p).astype(BF)

    total[...] = jnp.zeros_like(total)

    pltpu.make_async_copy(heard, heard, plsem.at[1]).wait()
    zx, gc = line & 15, line >> 4
    n_dy = ((gc >> 1) + (zx >> 2) + zx) & 3
    at = (n_dy * 4 + (zx >> 2)) * 8 + (zx & 3) * 2 + (gc & 1)
    order = onehot(iota((PEERS, PEERS), 1) == at)
    mine = mm(order, heard[...].astype(F32).reshape(PEERS, 128).astype(BF)).astype(BF)
    mine_t = mm_nt(eye128, mine).astype(BF)

    def take_enc(g, carry):
        receivers(mine_t, maps1, 0, g, r1, r1t)
        receivers(mine_t, maps2, 16, g, r2, r2t)
        picked = mm(r1[g], gathered[...])
        wait_group(g, recv1, rsem.at[0, g])
        rows, last = unpack_units(recv1, g)
        value_l, slope = gated(last + fold(picked[MAIN:]))
        d1l[g] = slope.astype(BF)
        value, slope = gated(rows + picked[:MAIN])
        d1[g] = slope.astype(BF)
        both = jnp.concatenate([value.astype(BF), unfold(value_l).astype(BF)], axis=0)
        total[...] += mm(r1t[g], both)
        return carry

    lax.fori_loop(0, GROUPS, take_enc, 0)

    for n in (4, 5, 12):
        loads[n].wait()
    enc_sum = total[...]
    enc_norm, enc_scale = norm_forward(enc_sum)
    hidden = mesh_ref[...].astype(F32) + mm(enc_norm.astype(BF), w_node[...])
    hidden_ref[...] = hidden
    hidden_bf = hidden.astype(BF)
    rows1[pl.ds(0, 128), :] = mm(hidden_bf, w_send[...]).astype(BF)

    def send_msh(g, carry):
        pack(send2, g, mm(a2[g], rows1[pl.ds(0, 128), :]))
        send_group(g, send2, recv2, ssem.at[1], rsem.at[1, g], 1)
        return carry

    lax.fori_loop(0, GROUPS, send_msh, 0)
    gathered[...] = mm(hidden_bf, w_recv[...]).astype(BF)
    cot_bf = cot[...]
    grad_norm = mm_nt(cot_bf, w_node[...]).astype(BF).astype(F32)
    total[...] = jnp.zeros_like(total)

    def take_msh(g, carry):
        picked = mm(r2[g], gathered[...])
        wait_group(g, recv2, rsem.at[1, g])
        value, slope = gated(unpack(recv2, g) + picked)
        d2[g] = slope.astype(BF)
        total[...] += mm(r2t[g], value.astype(BF))
        return carry

    lax.fori_loop(0, GROUPS, take_msh, 0)

    msh_sum = total[...]
    msh_norm, msh_scale = norm_forward(msh_sum)
    gathered[...] = norm_backward(grad_norm, msh_sum, msh_scale).astype(BF)

    def back_msh(g, carry):
        grad = mm(r2[g], gathered[...]) * d2[g].astype(F32)
        pack(back2, g, grad)
        send_group(g, back2, ret2, ssem.at[2], rsem.at[2, g], -1)
        d2[g] = grad.astype(BF)
        return carry

    lax.fori_loop(0, GROUPS, back_msh, 0)
    out_ref[...] = (hidden_ref[...] + mm(msh_norm.astype(BF), w_node[...])).astype(BF)
    total[...] = jnp.zeros_like(total)

    def sum_msh(g, carry):
        total[...] += mm(r2t[g], d2[g])
        return carry

    lax.fori_loop(0, GROUPS, sum_msh, 0)
    part = mm_nt(total[...].astype(BF), w_recv[...])
    total[...] = jnp.zeros_like(total)

    def take_back_msh(g, carry):
        wait_group(g, ret2, rsem.at[2, g])
        total[...] += mm(a2t[g], unpack(ret2, g).astype(BF))
        return carry

    lax.fori_loop(0, GROUPS, take_back_msh, 0)
    grad_hidden_bf = (part + mm_nt(total[...].astype(BF), w_send[...])).astype(BF)
    grad_hidden = (cot_bf.astype(F32) + grad_hidden_bf.astype(F32)).astype(BF)
    grad_norm1 = mm_nt(grad_hidden, w_node[...]).astype(BF).astype(F32)
    gathered[...] = norm_backward(grad_norm1, enc_sum, enc_scale).astype(BF)

    def back_enc(g, carry):
        picked = mm(r1[g], gathered[...])
        grad = picked[:MAIN] * d1[g].astype(F32)
        grad_l = fold(picked[MAIN:]) * d1l[g].astype(F32)
        pack_units(back1, g, grad, grad_l)
        send_group(g, back1, ret1, ssem.at[3], rsem.at[3, g], -1)
        d1[g] = grad.astype(BF)
        d1l[g] = grad_l.astype(BF)
        return carry

    lax.fori_loop(0, GROUPS, back_enc, 0)
    total[...] = jnp.zeros_like(total)

    def sum_enc(g, carry):
        both = jnp.concatenate([d1[g], unfold(d1l[g].astype(F32)).astype(BF)], axis=0)
        total[...] += mm(r1t[g], both)
        return carry

    lax.fori_loop(0, GROUPS, sum_enc, 0)
    mesh_part = mm_nt(total[...].astype(BF), w_recv[...]).astype(BF)
    mesh_grad[...] = (grad_hidden.astype(F32) + mesh_part.astype(F32)).astype(BF)

    def take_back_enc(g, carry):
        wait_group(g, ret1, rsem.at[3, g])
        rows, last = unpack_units(ret1, g)
        both = jnp.concatenate([rows.astype(BF), unfold(last).astype(BF)], axis=0)
        return carry + mm(a1t[g], both)

    grid_rows = lax.fori_loop(0, GROUPS, take_back_enc, jnp.zeros(grid_ref.shape, F32))
    grid_grad[...] = mm_nt(grid_rows.astype(BF), w_grid[...]).astype(BF)

    for src, sem in (
        (send1, ssem.at[0]),
        (send2, ssem.at[1]),
        (back2, ssem.at[2]),
        (back1, ssem.at[3]),
        (told, rlsem.at[0]),
        (plane_told, plsem.at[0]),
    ):
        at = src.at[pl.ds(1, src.shape[0] - 1)]
        pltpu.make_async_copy(at, at, sem).wait()


def hand_on(*refs):
    for n in range(3):
        refs[n + 3][...] = refs[n][...]


def body(*args):
    grid_latent, mesh_latent = args[:2]
    args = [v.reshape(1, -1) if n in (7, 10) else v for n, v in enumerate(args)]
    vmem = pl.BlockSpec(memory_space=pltpu.VMEM)
    anywhere = pl.BlockSpec(memory_space=pl.ANY)
    nodes, width = mesh_latent.shape
    grid_nodes = grid_latent.shape[0]

    def block(*shape):
        return pltpu.VMEM(shape, BF)

    scratch = [pltpu.VMEM(v.shape, v.dtype) for v in args]
    scratch += [
        block(PEERS, 9, 4, 128),
        block(PEERS, 9, 4, 128),
        block(PEERS, 48, 128),
        block(PEERS, 48, 128),
        block(PEERS, 48, 128),
        block(PEERS, 48, 128),
        block(PEERS, 9, 4, 128),
        block(PEERS, 9, 4, 128),
        block(GROUPS, ROWS1, grid_nodes),
        block(GROUPS, grid_nodes, ROWS1),
        block(GROUPS, ROWS2, nodes),
        block(GROUPS, nodes, ROWS2),
        block(GROUPS, ROWS1, nodes),
        block(GROUPS, nodes, ROWS1),
        block(GROUPS, ROWS2, nodes),
        block(GROUPS, nodes, ROWS2),
        block(GROUPS, MAIN, width),
        block(GROUPS, LAST, 128),
        block(GROUPS, ROWS2, width),
        block(8, 16, 128),
        block(8, 16, 128),
        block(16, 8, 128),
        block(16, 8, 128),
        block(grid_nodes, width),
        block(nodes, width),
        pltpu.VMEM((nodes, width), F32),
        pltpu.VMEM((nodes, width), F32),
        pltpu.SemaphoreType.DMA((13,)),
        pltpu.SemaphoreType.DMA((4,)),
        pltpu.SemaphoreType.DMA((4, GROUPS)),
        pltpu.SemaphoreType.DMA((2,)),
        pltpu.SemaphoreType.DMA((2,)),
        pltpu.SemaphoreType.REGULAR,
    ]
    results = pl.pallas_call(
        kernel,
        out_shape=(
            jax.ShapeDtypeStruct(mesh_latent.shape, BF),
            jax.ShapeDtypeStruct(grid_latent.shape, BF),
            jax.ShapeDtypeStruct(mesh_latent.shape, BF),
        ),
        in_specs=[anywhere] * 13,
        out_specs=[vmem] * 3,
        scratch_shapes=scratch,
        compiler_params=pltpu.CompilerParams(
            collective_id=0, has_side_effects=True, vmem_limit_bytes=56 << 20
        ),
    )(*args)
    return pl.pallas_call(
        hand_on,
        out_shape=[jax.ShapeDtypeStruct(v.shape, v.dtype) for v in results],
        in_specs=[vmem] * 3,
        out_specs=[vmem] * 3,
    )(*results)


def solution(mesh):
    rows = P(("gx", "gy"), None)
    flat = P(("gx", "gy"))
    placed = (rows, rows, P(), P(), P(), P(), flat, rows, flat, flat, rows, flat, rows)
    return jax.shard_map(
        body, mesh=mesh, in_specs=placed, out_specs=(rows, rows, rows), check_vma=False
    )
```

```python
import jax
import jax.numpy as jnp
from jax import lax
from jax.experimental import pallas as pl
from jax.experimental.pallas import tpu as pltpu
from jax.sharding import PartitionSpec as P

MESH = pl.DeviceIdType.MESH
BF = jnp.bfloat16
F32 = jnp.float32
I32 = jnp.int32

PEERS = 128
GROUPS = 8
SIZE = 16
MAIN = SIZE * 8
TAIL = SIZE * 4
LAST = SIZE * 8
ROWS1 = MAIN + LAST
ROWS2 = MAIN + TAIL
NEVER = 99
NEAR_LAST = sorted(range(SIZE), key=lambda k: -min(k // 4, 4 - k // 4) - min(k % 4, 4 - k % 4))


def coords():
    y = lax.axis_index("gx")
    g = lax.axis_index("gy")
    return y, g // 8, (g // 2) % 4, g % 2


def iota(shape, axis):
    return lax.broadcasted_iota(I32, shape, axis)


def onehot(mask):
    return jnp.where(mask, 1.0, 0.0).astype(BF)


def mm(a, b):
    return lax.dot_general(a, b, (((1,), (0,)), ((), ())), preferred_element_type=F32)


def mm_nt(a, b):
    return lax.dot_general(a, b, (((1,), (1,)), ((), ())), preferred_element_type=F32)


def quarter(v, q):
    return v[..., q * 128 : q * 128 + 128]


def swap(a, b):
    low = iota(a.shape, 1) < 4
    return jnp.where(low, a, pltpu.roll(b, 4, 1)), jnp.where(low, pltpu.roll(a, 4, 1), b)


def pack_main(wire, g, rows):
    at = pl.ds(g * SIZE, SIZE)
    m = [quarter(rows, q).reshape(SIZE, 8, 128) for q in range(4)]
    wire[at, 0:16, :] = jnp.concatenate([m[0], m[1]], axis=1).astype(BF)
    wire[at, 16:32, :] = jnp.concatenate([m[2], m[3]], axis=1).astype(BF)


def unpack_main(wire, g):
    at = pl.ds(g * SIZE, SIZE)
    a = wire[at, 0:16, :].astype(F32)
    b = wire[at, 16:32, :].astype(F32)
    parts = (a[:, :8], a[:, 8:], b[:, :8], b[:, 8:])
    return jnp.concatenate([v.reshape(MAIN, 128) for v in parts], axis=1)


def pack_units(wire, g, rows, last):
    at = pl.ds(g * SIZE, SIZE)
    for q in range(4):
        m = quarter(rows, q).reshape(SIZE, 8, 128)
        wire[at, 2 * q] = m[:, :4].astype(BF)
        wire[at, 2 * q + 1] = m[:, 4:].astype(BF)
    last = last.reshape(SIZE, 8, 128)
    wire[at, 8] = last[:, :4].astype(BF)


def unpack_units(wire, g):
    at = pl.ds(g * SIZE, SIZE)

    def pair(n):
        low = wire[at, n].astype(F32)
        high = wire[at, n + 1].astype(F32) if n + 1 < wire.shape[1] else jnp.zeros_like(low)
        return jnp.concatenate([low, high], axis=1).reshape(MAIN, 128)

    return jnp.concatenate([pair(2 * q) for q in range(4)], axis=1), pair(8)


def pack_tail(wire, g, rows):
    t = [quarter(rows, q).reshape(SIZE // 2, 8, 128) for q in range(4)]
    e01, o01 = swap(t[0], t[1])
    e23, o23 = swap(t[2], t[3])
    even = jnp.concatenate([e01, e23], axis=1)
    odd = jnp.concatenate([o01, o23], axis=1)
    both = jnp.stack([even, odd], axis=1).reshape(SIZE, 16, 128)
    wire[pl.ds(g * SIZE, SIZE), 32:48, :] = both.astype(BF)


def unpack_tail(wire, g):
    t = wire[pl.ds(g * SIZE, SIZE), 32:48, :].astype(F32).reshape(SIZE // 2, 2, 16, 128)
    even, odd = t[:, 0], t[:, 1]
    t0, t1 = swap(even[:, :8], odd[:, :8])
    t2, t3 = swap(even[:, 8:], odd[:, 8:])
    return jnp.concatenate([v.reshape(TAIL, 128) for v in (t0, t1, t2, t3)], axis=1)


def pack(wire, g, rows):
    pack_main(wire, g, rows[:MAIN])
    pack_tail(wire, g, rows[MAIN:])


def unpack(wire, g):
    return jnp.concatenate([unpack_main(wire, g), unpack_tail(wire, g)], axis=0)


def fold(rows):
    u = iota((LAST, 128), 0) & 7
    part = jnp.where(u == 2, quarter(rows, 2), quarter(rows, 3))
    return jnp.where(u == 0, quarter(rows, 0), jnp.where(u == 1, quarter(rows, 1), part))


def unfold(part):
    u = iota((LAST, 128), 0) & 7
    return jnp.concatenate([jnp.where(u == q, part, 0.0) for q in range(4)], axis=1)


def norm_forward(total):
    scale = lax.rsqrt(jnp.mean(total * total, axis=-1, keepdims=True) + 1e-05)
    return total * scale, scale


def norm_backward(grad, total, scale):
    inner = jnp.mean(grad * total, axis=-1, keepdims=True)
    return scale * (grad - total * (scale * scale * inner))


def gated(pre):
    gate = 0.5 * jnp.tanh(0.5 * pre) + 0.5
    value = pre * gate
    return value, gate + value * (1.0 - gate)


def kernel(*refs):
    inputs, refs = refs[:13], refs[13:]
    (out_ref, grid_grad, mesh_grad), refs = refs[:3], refs[3:]
    local, refs = refs[:13], refs[13:]
    grid_ref, mesh_ref, w_grid, w_recv, w_send, w_node, es, eo, et, ms, mo, mt, cot = local
    (
        send1, recv1, send2, recv2, back2, ret2, back1, ret1,
        a1, a1t, a2, a2t, r1, r1t, r2, r2t, d1, d1l, d2,
        told, ring_told, plane_told, heard, rows1, gathered, total, hidden_ref,
        isem, ssem, rsem, rlsem, plsem, psem,
    ) = refs

    y, z, x, c = coords()

    barrier = pltpu.get_barrier_semaphore()
    ring = [(y, z * 8 + ((x + d // 2) % 4) * 2 + (c + d) % 2) for d in range(1, 8)]
    plane = [((y + d // 4) % 4, ((z + d) % 4) * 8 + x * 2 + c) for d in range(1, 16)]

    def greet(sem, ring):
        for device in ring:
            pl.semaphore_signal(sem, inc=1, device_id=device, device_id_type=MESH)

    far = sorted(range(1, 64), key=lambda i: -sum(min(d, 4 - d) for d in (i // 16, i // 4 % 4, i % 4)))
    like = [((y + i // 16) % 4, ((z + i // 4) % 4) * 8 + ((x + i) % 4) * 2 + c) for i in far]
    twin = [(y, z * 8 + x * 2 + 1 - c)]
    greet(barrier, like + twin)

    loads = [pltpu.make_async_copy(a, b, isem.at[n]) for n, (a, b) in enumerate(zip(inputs, local))]
    order = (7, 10, 8, 11, 6, 9, 0, 2, 1, 3, 5, 4, 12)
    for n in order:
        loads[n].start()

    def route(owner):
        edges = owner.shape[1]
        dy = ((owner >> 5) - y) & 3
        dz = (((owner >> 3) & 3) - z) & 3
        dx = (((owner >> 1) & 3) - x) & 3
        dc = ((owner & 1) - c) & 1
        j = (((dy - dz - dx) & 3) * 2 + dc) * SIZE + dz * 4 + dx
        same = iota((PEERS, edges), 0) == (dx * 2 + dc) * 16 + dy * 4 + dz
        before = onehot(iota((edges, edges), 0) < iota((edges, edges), 1))
        count = mm(onehot(same), before)
        rank = jnp.sum(jnp.where(same, count, 0.0), axis=0, keepdims=True).astype(I32)
        return j, rank, onehot(same)

    def labels(rank, target, base):
        at = iota((128, rank.shape[1]), 0) == rank + base
        return jnp.where(at, (target + 1).astype(F32), 0.0).astype(BF)

    for n in (7, 10, 8, 11):
        loads[n].wait()
    j1, k1, same1 = route(eo[...])
    j2, k2, same2 = route(mo[...])
    told[...] = (
        mm_nt(same1, labels(k1, et[...].reshape(1, -1), 0)) + mm_nt(same2, labels(k2, mt[...].reshape(1, -1), 16))
    ).astype(BF).reshape(8, 16, 128)

    loads[6].wait()
    edges1 = j1.shape[1]
    q1 = onehot(iota((grid_ref.shape[0], edges1), 0) == es[...].reshape(1, -1))
    main1 = jnp.where(k1 < 8, j1 * 8 + k1, -1)
    last1_of = jnp.where(k1 == 8, j1, -1)
    row1 = iota((MAIN, edges1), 0)
    def places1(g):
        p_main = onehot(row1 + g * MAIN == main1)
        p_last = onehot(jnp.where((row1 & 7) < 4, (row1 >> 3) + g * SIZE, -2) == last1_of)
        return jnp.concatenate([p_main, p_last], axis=0)

    for g in range(GROUPS):
        a1[g] = mm_nt(places1(g), q1).astype(BF)

    for n in (0, 2):
        loads[n].wait()
    rows1[...] = mm(grid_ref[...], w_grid[...]).astype(BF)
    for n in (1, 3):
        loads[n].wait()
    gathered[...] = mm(mesh_ref[...], w_recv[...]).astype(BF)

    pl.semaphore_wait(barrier, 64)
    greet(psem, twin)
    pl.semaphore_wait(psem, 1)

    def pass_on(src, dst, sem, devices):
        pltpu.make_async_copy(src.at[0], dst.at[0], sem.at[1]).start()
        for n, device in enumerate(devices):
            pltpu.make_async_remote_copy(
                src.at[n + 1], dst.at[n + 1], sem.at[0], sem.at[1], device_id=device, device_id_type=MESH
            ).start()

    pass_on(told, ring_told, rlsem, ring)

    def send_group(g, src, dst, s, r, sign):
        gh, gl = g // 2, g % 2
        tc = (c + gl) % 2
        ty = [(y + sign * (gh + m) + 8) % 4 for m in range(4)]
        for k in NEAR_LAST:
            kz, kx = k // 4, k % 4
            tz, tx = (z + sign * kz + 4) % 4, (x + sign * kx + 4) % 4
            device = (ty[(kz + kx) % 4], tz * 8 + tx * 2 + tc)
            j = g * SIZE + k

            def remote():
                pltpu.make_async_remote_copy(
                    src.at[j], dst.at[j], s, r, device_id=device, device_id_type=MESH
                ).start()

            def mine():
                pltpu.make_async_copy(src.at[j], dst.at[j], r).start()

            if k == 0:
                pl.when(g > 0)(remote)
                pl.when(g == 0)(mine)
            else:
                remote()

    def wait_group(g, dst, sem):
        at = dst.at[pl.ds(g * SIZE, SIZE)]
        pltpu.make_async_copy(at, at, sem).wait()

    eye128 = onehot(iota((128, 128), 0) == iota((128, 128), 1))

    def slot_maps(rows):
        s = iota((1, rows), 1)
        if rows == ROWS1:
            peer = (s & (MAIN - 1)) >> 3
            rank = jnp.where(s < MAIN, s & 7, jnp.where((s & 7) < 4, 8, NEVER))
        else:
            peer = jnp.where(s < MAIN, s >> 3, (s - MAIN) >> 2)
            rank = jnp.where(s < MAIN, s & 7, 8 + (s & 3))
        eye = onehot(iota((rows, rows), 0) == iota((rows, rows), 1))
        return peer, rank, eye

    maps1 = slot_maps(ROWS1)
    maps2 = slot_maps(ROWS2)

    def receivers(mine_t, maps, base, g, r, rt):
        peer, rank, eye = maps
        lines = mm(mine_t, onehot(iota((PEERS, rank.shape[1]), 0) == peer + g * SIZE))
        lane = iota(lines.shape, 0)
        row = jnp.sum(jnp.where(lane == rank + base, lines, 0.0), axis=0, keepdims=True)
        flag = onehot(row.astype(I32) == lane + 1)
        rt[g] = flag
        r[g] = mm_nt(eye, flag).astype(BF)

    def send_enc(g, carry):
        rows = mm(a1[g], rows1[...])
        pack_units(send1, g, rows[:MAIN], fold(rows[MAIN:]))
        send_group(g, send1, recv1, ssem.at[0], rsem.at[0, g], 1)
        return carry

    lax.fori_loop(0, 2, send_enc, 0)

    pltpu.make_async_copy(ring_told, ring_told, rlsem.at[1]).wait()
    line = iota((PEERS, PEERS), 0)
    turn = onehot(iota((PEERS, PEERS), 1) == (line & 7) * 16 + (line >> 3))
    plane_told[...] = mm(turn, ring_told[...].reshape(PEERS, 128)).reshape(16, 8, 128).astype(BF)
    pass_on(plane_told, heard, plsem, plane)

    lax.fori_loop(2, GROUPS, send_enc, 0)

    for g in range(GROUPS):
        a1t[g] = mm_nt(q1, places1(g)).astype(BF)
    for n in (9,):
        loads[n].wait()
    edges2 = j2.shape[1]
    q2 = onehot(iota((mesh_ref.shape[0], edges2), 0) == ms[...].reshape(1, -1))
    inside2 = jnp.where(k2 < 8, (j2 & 15) * 8 + k2, MAIN + (j2 & 15) * 4 + k2 - 8)
    place2 = (j2 >> 4) * ROWS2 + inside2
    for g in range(GROUPS):
        p = onehot(iota((ROWS2, edges2), 0) + g * ROWS2 == place2)
        a2[g] = mm_nt(p, q2).astype(BF)
        a2t[g] = mm_nt(q2, p).astype(BF)

    total[...] = jnp.zeros_like(total)

    pltpu.make_async_copy(heard, heard, plsem.at[1]).wait()
    zx, gc = line & 15, line >> 4
    n_dy = ((gc >> 1) + (zx >> 2) + zx) & 3
    at = (n_dy * 4 + (zx >> 2)) * 8 + (zx & 3) * 2 + (gc & 1)
    order = onehot(iota((PEERS, PEERS), 1) == at)
    mine = mm(order, heard[...].astype(F32).reshape(PEERS, 128).astype(BF)).astype(BF)
    mine_t = mm_nt(eye128, mine).astype(BF)

    def take_enc(g, carry):
        receivers(mine_t, maps1, 0, g, r1, r1t)
        receivers(mine_t, maps2, 16, g, r2, r2t)
        picked = mm(r1[g], gathered[...])
        wait_group(g, recv1, rsem.at[0, g])
        rows, last = unpack_units(recv1, g)
        value_l, slope = gated(last + fold(picked[MAIN:]))
        d1l[g] = slope.astype(BF)
        value, slope = gated(rows + picked[:MAIN])
        d1[g] = slope.astype(BF)
        both = jnp.concatenate([value.astype(BF), unfold(value_l).astype(BF)], axis=0)
        total[...] += mm(r1t[g], both)
        return carry

    lax.fori_loop(0, GROUPS, take_enc, 0)

    for n in (4, 5, 12):
        loads[n].wait()
    enc_sum = total[...]
    enc_norm, enc_scale = norm_forward(enc_sum)
    hidden = mesh_ref[...].astype(F32) + mm(enc_norm.astype(BF), w_node[...])
    hidden_ref[...] = hidden
    hidden_bf = hidden.astype(BF)
    rows1[pl.ds(0, 128), :] = mm(hidden_bf, w_send[...]).astype(BF)

    def send_msh(g, carry):
        pack(send2, g, mm(a2[g], rows1[pl.ds(0, 128), :]))
        send_group(g, send2, recv2, ssem.at[1], rsem.at[1, g], 1)
        return carry

    lax.fori_loop(0, GROUPS, send_msh, 0)
    gathered[...] = mm(hidden_bf, w_recv[...]).astype(BF)
    cot_bf = cot[...]
    grad_norm = mm_nt(cot_bf, w_node[...]).astype(BF).astype(F32)
    total[...] = jnp.zeros_like(total)

    def take_msh(g, carry):
        picked = mm(r2[g], gathered[...])
        wait_group(g, recv2, rsem.at[1, g])
        value, slope = gated(unpack(recv2, g) + picked)
        d2[g] = slope.astype(BF)
        total[...] += mm(r2t[g], value.astype(BF))
        return carry

    lax.fori_loop(0, GROUPS, take_msh, 0)

    msh_sum = total[...]
    msh_norm, msh_scale = norm_forward(msh_sum)
    gathered[...] = norm_backward(grad_norm, msh_sum, msh_scale).astype(BF)

    def back_msh(g, carry):
        grad = mm(r2[g], gathered[...]) * d2[g].astype(F32)
        pack(back2, g, grad)
        send_group(g, back2, ret2, ssem.at[2], rsem.at[2, g], -1)
        d2[g] = grad.astype(BF)
        return carry

    lax.fori_loop(0, GROUPS, back_msh, 0)
    out_ref[...] = (hidden_ref[...] + mm(msh_norm.astype(BF), w_node[...])).astype(BF)
    total[...] = jnp.zeros_like(total)

    def sum_msh(g, carry):
        total[...] += mm(r2t[g], d2[g])
        return carry

    lax.fori_loop(0, GROUPS, sum_msh, 0)
    part = mm_nt(total[...].astype(BF), w_recv[...])
    total[...] = jnp.zeros_like(total)

    def take_back_msh(g, carry):
        wait_group(g, ret2, rsem.at[2, g])
        total[...] += mm(a2t[g], unpack(ret2, g).astype(BF))
        return carry

    lax.fori_loop(0, GROUPS, take_back_msh, 0)
    grad_hidden_bf = (part + mm_nt(total[...].astype(BF), w_send[...])).astype(BF)
    grad_hidden = (cot_bf.astype(F32) + grad_hidden_bf.astype(F32)).astype(BF)
    grad_norm1 = mm_nt(grad_hidden, w_node[...]).astype(BF).astype(F32)
    gathered[...] = norm_backward(grad_norm1, enc_sum, enc_scale).astype(BF)

    def back_enc(g, carry):
        picked = mm(r1[g], gathered[...])
        grad = picked[:MAIN] * d1[g].astype(F32)
        grad_l = fold(picked[MAIN:]) * d1l[g].astype(F32)
        pack_units(back1, g, grad, grad_l)
        send_group(g, back1, ret1, ssem.at[3], rsem.at[3, g], -1)
        d1[g] = grad.astype(BF)
        d1l[g] = grad_l.astype(BF)
        return carry

    lax.fori_loop(0, GROUPS, back_enc, 0)
    total[...] = jnp.zeros_like(total)

    def sum_enc(g, carry):
        both = jnp.concatenate([d1[g], unfold(d1l[g].astype(F32)).astype(BF)], axis=0)
        total[...] += mm(r1t[g], both)
        return carry

    lax.fori_loop(0, GROUPS, sum_enc, 0)
    mesh_part = mm_nt(total[...].astype(BF), w_recv[...]).astype(BF)
    mesh_grad[...] = (grad_hidden.astype(F32) + mesh_part.astype(F32)).astype(BF)

    def take_back_enc(g, carry):
        wait_group(g, ret1, rsem.at[3, g])
        rows, last = unpack_units(ret1, g)
        both = jnp.concatenate([rows.astype(BF), unfold(last).astype(BF)], axis=0)
        return carry + mm(a1t[g], both)

    grid_rows = lax.fori_loop(0, GROUPS, take_back_enc, jnp.zeros(grid_ref.shape, F32))
    grid_grad[...] = mm_nt(grid_rows.astype(BF), w_grid[...]).astype(BF)

    for src, sem in (
        (send1, ssem.at[0]),
        (send2, ssem.at[1]),
        (back2, ssem.at[2]),
        (back1, ssem.at[3]),
        (told, rlsem.at[0]),
        (plane_told, plsem.at[0]),
    ):
        at = src.at[pl.ds(1, src.shape[0] - 1)]
        pltpu.make_async_copy(at, at, sem).wait()


def hand_on(*refs):
    for n in range(3):
        refs[n + 3][...] = refs[n][...]


def body(*args):
    grid_latent, mesh_latent = args[:2]
    args = [v.reshape(1, -1) if n in (7, 10) else v for n, v in enumerate(args)]
    vmem = pl.BlockSpec(memory_space=pltpu.VMEM)
    anywhere = pl.BlockSpec(memory_space=pl.ANY)
    nodes, width = mesh_latent.shape
    grid_nodes = grid_latent.shape[0]

    def block(*shape):
        return pltpu.VMEM(shape, BF)

    scratch = [pltpu.VMEM(v.shape, v.dtype) for v in args]
    scratch += [
        block(PEERS, 9, 4, 128),
        block(PEERS, 9, 4, 128),
        block(PEERS, 48, 128),
        block(PEERS, 48, 128),
        block(PEERS, 48, 128),
        block(PEERS, 48, 128),
        block(PEERS, 9, 4, 128),
        block(PEERS, 9, 4, 128),
        block(GROUPS, ROWS1, grid_nodes),
        block(GROUPS, grid_nodes, ROWS1),
        block(GROUPS, ROWS2, nodes),
        block(GROUPS, nodes, ROWS2),
        block(GROUPS, ROWS1, nodes),
        block(GROUPS, nodes, ROWS1),
        block(GROUPS, ROWS2, nodes),
        block(GROUPS, nodes, ROWS2),
        block(GROUPS, MAIN, width),
        block(GROUPS, LAST, 128),
        block(GROUPS, ROWS2, width),
        block(8, 16, 128),
        block(8, 16, 128),
        block(16, 8, 128),
        block(16, 8, 128),
        block(grid_nodes, width),
        block(nodes, width),
        pltpu.VMEM((nodes, width), F32),
        pltpu.VMEM((nodes, width), F32),
        pltpu.SemaphoreType.DMA((13,)),
        pltpu.SemaphoreType.DMA((4,)),
        pltpu.SemaphoreType.DMA((4, GROUPS)),
        pltpu.SemaphoreType.DMA((2,)),
        pltpu.SemaphoreType.DMA((2,)),
        pltpu.SemaphoreType.REGULAR,
    ]
    results = pl.pallas_call(
        kernel,
        out_shape=(
            jax.ShapeDtypeStruct(mesh_latent.shape, BF),
            jax.ShapeDtypeStruct(grid_latent.shape, BF),
            jax.ShapeDtypeStruct(mesh_latent.shape, BF),
        ),
        in_specs=[anywhere] * 13,
        out_specs=[vmem] * 3,
        scratch_shapes=scratch,
        compiler_params=pltpu.CompilerParams(
            collective_id=0, has_side_effects=True, vmem_limit_bytes=56 << 20
        ),
    )(*args)
    return pl.pallas_call(
        hand_on,
        out_shape=[jax.ShapeDtypeStruct(v.shape, v.dtype) for v in results],
        in_specs=[vmem] * 3,
        out_specs=[vmem] * 3,
    )(*results)


def solution(mesh):
    rows = P(("gx", "gy"), None)
    flat = P(("gx", "gy"))
    placed = (rows, rows, P(), P(), P(), P(), flat, rows, flat, flat, rows, flat, rows)
    return jax.shard_map(
        body, mesh=mesh, in_specs=placed, out_specs=(rows, rows, rows), check_vma=False
    )
```

```python
import jax
import jax.numpy as jnp
from jax import lax
from jax.experimental import pallas as pl
from jax.experimental.pallas import tpu as pltpu
from jax.sharding import PartitionSpec as P

MESH = pl.DeviceIdType.MESH
BF = jnp.bfloat16
F32 = jnp.float32
I32 = jnp.int32

PEERS = 128
GROUPS = 8
SIZE = 16
MAIN = SIZE * 8
TAIL = SIZE * 4
LAST = SIZE * 8
ROWS1 = MAIN + LAST
ROWS2 = MAIN + TAIL
NEVER = 99
NEAR_LAST = sorted(range(SIZE), key=lambda k: -min(k // 4, 4 - k // 4) - min(k % 4, 4 - k % 4))


def coords():
    y = lax.axis_index("gx")
    g = lax.axis_index("gy")
    return y, g // 8, (g // 2) % 4, g % 2


def iota(shape, axis):
    return lax.broadcasted_iota(I32, shape, axis)


def onehot(mask):
    return jnp.where(mask, 1.0, 0.0).astype(BF)


def mm(a, b):
    return lax.dot_general(a, b, (((1,), (0,)), ((), ())), preferred_element_type=F32)


def mm_nt(a, b):
    return lax.dot_general(a, b, (((1,), (1,)), ((), ())), preferred_element_type=F32)


def quarter(v, q):
    return v[..., q * 128 : q * 128 + 128]


def swap(a, b):
    low = iota(a.shape, 1) < 4
    return jnp.where(low, a, pltpu.roll(b, 4, 1)), jnp.where(low, pltpu.roll(a, 4, 1), b)


def pack_main(wire, g, rows):
    at = pl.ds(g * SIZE, SIZE)
    m = [quarter(rows, q).reshape(SIZE, 8, 128) for q in range(4)]
    wire[at, 0:16, :] = jnp.concatenate([m[0], m[1]], axis=1).astype(BF)
    wire[at, 16:32, :] = jnp.concatenate([m[2], m[3]], axis=1).astype(BF)


def unpack_main(wire, g):
    at = pl.ds(g * SIZE, SIZE)
    a = wire[at, 0:16, :].astype(F32)
    b = wire[at, 16:32, :].astype(F32)
    parts = (a[:, :8], a[:, 8:], b[:, :8], b[:, 8:])
    return jnp.concatenate([v.reshape(MAIN, 128) for v in parts], axis=1)


def pack_units(wire, g, rows, last):
    at = pl.ds(g * SIZE, SIZE)
    for q in range(4):
        m = quarter(rows, q).reshape(SIZE, 8, 128)
        wire[at, 2 * q] = m[:, :4].astype(BF)
        wire[at, 2 * q + 1] = m[:, 4:].astype(BF)
    last = last.reshape(SIZE, 8, 128)
    wire[at, 8] = last[:, :4].astype(BF)


def unpack_units(wire, g):
    at = pl.ds(g * SIZE, SIZE)

    def pair(n):
        low = wire[at, n].astype(F32)
        high = wire[at, n + 1].astype(F32) if n + 1 < wire.shape[1] else jnp.zeros_like(low)
        return jnp.concatenate([low, high], axis=1).reshape(MAIN, 128)

    return jnp.concatenate([pair(2 * q) for q in range(4)], axis=1), pair(8)


def pack_tail(wire, g, rows):
    t = [quarter(rows, q).reshape(SIZE // 2, 8, 128) for q in range(4)]
    e01, o01 = swap(t[0], t[1])
    e23, o23 = swap(t[2], t[3])
    even = jnp.concatenate([e01, e23], axis=1)
    odd = jnp.concatenate([o01, o23], axis=1)
    both = jnp.stack([even, odd], axis=1).reshape(SIZE, 16, 128)
    wire[pl.ds(g * SIZE, SIZE), 32:48, :] = both.astype(BF)


def unpack_tail(wire, g):
    t = wire[pl.ds(g * SIZE, SIZE), 32:48, :].astype(F32).reshape(SIZE // 2, 2, 16, 128)
    even, odd = t[:, 0], t[:, 1]
    t0, t1 = swap(even[:, :8], odd[:, :8])
    t2, t3 = swap(even[:, 8:], odd[:, 8:])
    return jnp.concatenate([v.reshape(TAIL, 128) for v in (t0, t1, t2, t3)], axis=1)


def pack(wire, g, rows):
    pack_main(wire, g, rows[:MAIN])
    pack_tail(wire, g, rows[MAIN:])


def unpack(wire, g):
    return jnp.concatenate([unpack_main(wire, g), unpack_tail(wire, g)], axis=0)


def fold(rows):
    u = iota((LAST, 128), 0) & 7
    part = jnp.where(u == 2, quarter(rows, 2), quarter(rows, 3))
    return jnp.where(u == 0, quarter(rows, 0), jnp.where(u == 1, quarter(rows, 1), part))


def unfold(part):
    u = iota((LAST, 128), 0) & 7
    return jnp.concatenate([jnp.where(u == q, part, 0.0) for q in range(4)], axis=1)


def norm_forward(total):
    scale = lax.rsqrt(jnp.mean(total * total, axis=-1, keepdims=True) + 1e-05)
    return total * scale, scale


def norm_backward(grad, total, scale):
    inner = jnp.mean(grad * total, axis=-1, keepdims=True)
    return scale * (grad - total * (scale * scale * inner))


def gated(pre):
    gate = 0.5 * jnp.tanh(0.5 * pre) + 0.5
    value = pre * gate
    return value, gate + value * (1.0 - gate)


def kernel(*refs):
    inputs, refs = refs[:13], refs[13:]
    (out_ref, grid_grad, mesh_grad), refs = refs[:3], refs[3:]
    local, refs = refs[:13], refs[13:]
    grid_ref, mesh_ref, w_grid, w_recv, w_send, w_node, es, eo, et, ms, mo, mt, cot = local
    (
        send1, recv1, send2, recv2, back2, ret2, back1, ret1,
        a1, a1t, a2, a2t, r1, r1t, r2, r2t, d1, d1l, d2,
        told, ring_told, plane_told, heard, rows1, gathered, total, hidden_ref, grid_sum,
        isem, ssem, rsem, rlsem, plsem, psem,
    ) = refs

    y, z, x, c = coords()

    barrier = pltpu.get_barrier_semaphore()
    ring = [(y, z * 8 + ((x + d // 2) % 4) * 2 + (c + d) % 2) for d in range(1, 8)]
    plane = [((y + d // 4) % 4, ((z + d) % 4) * 8 + x * 2 + c) for d in range(1, 16)]

    def greet(sem, ring):
        for device in ring:
            pl.semaphore_signal(sem, inc=1, device_id=device, device_id_type=MESH)

    far = sorted(range(1, 64), key=lambda i: -sum(min(d, 4 - d) for d in (i // 16, i // 4 % 4, i % 4)))
    like = [((y + i // 16) % 4, ((z + i // 4) % 4) * 8 + ((x + i) % 4) * 2 + c) for i in far]
    twin = [(y, z * 8 + x * 2 + 1 - c)]
    greet(barrier, like + twin)

    loads = [pltpu.make_async_copy(a, b, isem.at[n]) for n, (a, b) in enumerate(zip(inputs, local))]
    order = (7, 10, 8, 11, 6, 9, 0, 2, 1, 3, 5, 4, 12)
    for n in order:
        loads[n].start()

    def route(owner):
        edges = owner.shape[1]
        dy = ((owner >> 5) - y) & 3
        dz = (((owner >> 3) & 3) - z) & 3
        dx = (((owner >> 1) & 3) - x) & 3
        dc = ((owner & 1) - c) & 1
        j = (((dy - dz - dx) & 3) * 2 + dc) * SIZE + dz * 4 + dx
        same = iota((PEERS, edges), 0) == (dx * 2 + dc) * 16 + dy * 4 + dz
        before = onehot(iota((edges, edges), 0) < iota((edges, edges), 1))
        count = mm(onehot(same), before)
        rank = jnp.sum(jnp.where(same, count, 0.0), axis=0, keepdims=True).astype(I32)
        return j, rank, onehot(same)

    def labels(rank, target, base):
        at = iota((128, rank.shape[1]), 0) == rank + base
        return jnp.where(at, (target + 1).astype(F32), 0.0).astype(BF)

    for n in (7, 10, 8, 11):
        loads[n].wait()
    j1, k1, same1 = route(eo[...])
    j2, k2, same2 = route(mo[...])
    told[...] = (
        mm_nt(same1, labels(k1, et[...].reshape(1, -1), 0)) + mm_nt(same2, labels(k2, mt[...].reshape(1, -1), 16))
    ).astype(BF).reshape(8, 16, 128)

    loads[6].wait()
    edges1 = j1.shape[1]
    q1 = onehot(iota((grid_ref.shape[0], edges1), 0) == es[...].reshape(1, -1))
    main1 = jnp.where(k1 < 8, j1 * 8 + k1, -1)
    last1_of = jnp.where(k1 == 8, j1, -1)
    row1 = iota((MAIN, edges1), 0)
    def places1(g):
        p_main = onehot(row1 + g * MAIN == main1)
        p_last = onehot(jnp.where((row1 & 7) < 4, (row1 >> 3) + g * SIZE, -2) == last1_of)
        return jnp.concatenate([p_main, p_last], axis=0)

    for g in range(GROUPS):
        a1[g] = mm_nt(places1(g), q1).astype(BF)

    for n in (0, 2):
        loads[n].wait()
    rows1[...] = mm(grid_ref[...], w_grid[...]).astype(BF)
    for n in (1, 3):
        loads[n].wait()
    gathered[...] = mm(mesh_ref[...], w_recv[...]).astype(BF)

    pl.semaphore_wait(barrier, 64)
    greet(psem, twin)
    pl.semaphore_wait(psem, 1)

    def pass_on(src, dst, sem, devices):
        pltpu.make_async_copy(src.at[0], dst.at[0], sem.at[1]).start()
        for n, device in enumerate(devices):
            pltpu.make_async_remote_copy(
                src.at[n + 1], dst.at[n + 1], sem.at[0], sem.at[1], device_id=device, device_id_type=MESH
            ).start()

    pass_on(told, ring_told, rlsem, ring)

    def send_group(g, src, dst, s, r, sign):
        gh, gl = g // 2, g % 2
        tc = (c + gl) % 2
        ty = [(y + sign * (gh + m) + 8) % 4 for m in range(4)]
        for k in NEAR_LAST:
            kz, kx = k // 4, k % 4
            tz, tx = (z + sign * kz + 4) % 4, (x + sign * kx + 4) % 4
            device = (ty[(kz + kx) % 4], tz * 8 + tx * 2 + tc)
            j = g * SIZE + k

            def remote():
                pltpu.make_async_remote_copy(
                    src.at[j], dst.at[j], s, r, device_id=device, device_id_type=MESH
                ).start()

            def mine():
                pltpu.make_async_copy(src.at[j], dst.at[j], r).start()

            if k == 0:
                pl.when(g > 0)(remote)
                pl.when(g == 0)(mine)
            else:
                remote()

    def wait_group(g, dst, sem):
        at = dst.at[pl.ds(g * SIZE, SIZE)]
        pltpu.make_async_copy(at, at, sem).wait()

    eye128 = onehot(iota((128, 128), 0) == iota((128, 128), 1))

    def slot_maps(rows):
        s = iota((1, rows), 1)
        if rows == ROWS1:
            peer = (s & (MAIN - 1)) >> 3
            rank = jnp.where(s < MAIN, s & 7, jnp.where((s & 7) < 4, 8, NEVER))
        else:
            peer = jnp.where(s < MAIN, s >> 3, (s - MAIN) >> 2)
            rank = jnp.where(s < MAIN, s & 7, 8 + (s & 3))
        eye = onehot(iota((rows, rows), 0) == iota((rows, rows), 1))
        return peer, rank, eye

    maps1 = slot_maps(ROWS1)
    maps2 = slot_maps(ROWS2)

    def receivers(mine_t, maps, base, g, r, rt):
        peer, rank, eye = maps
        lines = mm(mine_t, onehot(iota((PEERS, rank.shape[1]), 0) == peer + g * SIZE))
        lane = iota(lines.shape, 0)
        row = jnp.sum(jnp.where(lane == rank + base, lines, 0.0), axis=0, keepdims=True)
        flag = onehot(row.astype(I32) == lane + 1)
        rt[g] = flag
        r[g] = mm_nt(eye, flag).astype(BF)

    def send_enc(g, carry):
        rows = mm(a1[g], rows1[...])
        pack_units(send1, g, rows[:MAIN], fold(rows[MAIN:]))
        send_group(g, send1, recv1, ssem.at[0], rsem.at[0, g], 1)
        return carry

    lax.fori_loop(0, 2, send_enc, 0)

    pltpu.make_async_copy(ring_told, ring_told, rlsem.at[1]).wait()
    line = iota((PEERS, PEERS), 0)
    turn = onehot(iota((PEERS, PEERS), 1) == (line & 7) * 16 + (line >> 3))
    plane_told[...] = mm(turn, ring_told[...].reshape(PEERS, 128)).reshape(16, 8, 128).astype(BF)
    pass_on(plane_told, heard, plsem, plane)

    lax.fori_loop(2, GROUPS, send_enc, 0)

    for g in range(GROUPS):
        a1t[g] = mm_nt(q1, places1(g)).astype(BF)
    for n in (9,):
        loads[n].wait()
    edges2 = j2.shape[1]
    q2 = onehot(iota((mesh_ref.shape[0], edges2), 0) == ms[...].reshape(1, -1))
    inside2 = jnp.where(k2 < 8, (j2 & 15) * 8 + k2, MAIN + (j2 & 15) * 4 + k2 - 8)
    place2 = (j2 >> 4) * ROWS2 + inside2
    for g in range(GROUPS):
        p = onehot(iota((ROWS2, edges2), 0) + g * ROWS2 == place2)
        a2[g] = mm_nt(p, q2).astype(BF)
        a2t[g] = mm_nt(q2, p).astype(BF)

    total[...] = jnp.zeros_like(total)

    pltpu.make_async_copy(heard, heard, plsem.at[1]).wait()
    zx, gc = line & 15, line >> 4
    n_dy = ((gc >> 1) + (zx >> 2) + zx) & 3
    at = (n_dy * 4 + (zx >> 2)) * 8 + (zx & 3) * 2 + (gc & 1)
    order = onehot(iota((PEERS, PEERS), 1) == at)
    mine = mm(order, heard[...].astype(F32).reshape(PEERS, 128).astype(BF)).astype(BF)
    mine_t = mm_nt(eye128, mine).astype(BF)

    def take_enc(g, carry):
        receivers(mine_t, maps1, 0, g, r1, r1t)
        receivers(mine_t, maps2, 16, g, r2, r2t)
        picked = mm(r1[g], gathered[...])
        wait_group(g, recv1, rsem.at[0, g])
        rows, last = unpack_units(recv1, g)
        value_l, slope = gated(last + fold(picked[MAIN:]))
        d1l[g] = slope.astype(BF)
        value, slope = gated(rows + picked[:MAIN])
        d1[g] = slope.astype(BF)
        both = jnp.concatenate([value.astype(BF), unfold(value_l).astype(BF)], axis=0)
        total[...] += mm(r1t[g], both)
        return carry

    lax.fori_loop(0, GROUPS, take_enc, 0)

    for n in (4, 5, 12):
        loads[n].wait()
    enc_sum = total[...]
    enc_norm, enc_scale = norm_forward(enc_sum)
    hidden = mesh_ref[...].astype(F32) + mm(enc_norm.astype(BF), w_node[...])
    hidden_ref[...] = hidden
    hidden_bf = hidden.astype(BF)
    rows1[pl.ds(0, 128), :] = mm(hidden_bf, w_send[...]).astype(BF)

    def send_msh(g, carry):
        pack(send2, g, mm(a2[g], rows1[pl.ds(0, 128), :]))
        send_group(g, send2, recv2, ssem.at[1], rsem.at[1, g], 1)
        return carry

    lax.fori_loop(0, GROUPS, send_msh, 0)
    gathered[...] = mm(hidden_bf, w_recv[...]).astype(BF)
    cot_bf = cot[...]
    grad_norm = mm_nt(cot_bf, w_node[...]).astype(BF).astype(F32)
    total[...] = jnp.zeros_like(total)

    def take_msh(g, carry):
        picked = mm(r2[g], gathered[...])
        wait_group(g, recv2, rsem.at[1, g])
        value, slope = gated(unpack(recv2, g) + picked)
        d2[g] = slope.astype(BF)
        total[...] += mm(r2t[g], value.astype(BF))
        return carry

    lax.fori_loop(0, GROUPS, take_msh, 0)

    msh_sum = total[...]
    msh_norm, msh_scale = norm_forward(msh_sum)
    gathered[...] = norm_backward(grad_norm, msh_sum, msh_scale).astype(BF)

    def back_msh(g, carry):
        grad = mm(r2[g], gathered[...]) * d2[g].astype(F32)
        pack(back2, g, grad)
        send_group(g, back2, ret2, ssem.at[2], rsem.at[2, g], -1)
        d2[g] = grad.astype(BF)
        return carry

    lax.fori_loop(0, GROUPS, back_msh, 0)
    out_ref[...] = (hidden_ref[...] + mm(msh_norm.astype(BF), w_node[...])).astype(BF)
    total[...] = jnp.zeros_like(total)

    def sum_msh(g, carry):
        total[...] += mm(r2t[g], d2[g])
        return carry

    lax.fori_loop(0, GROUPS, sum_msh, 0)
    part = mm_nt(total[...].astype(BF), w_recv[...])
    total[...] = jnp.zeros_like(total)

    def take_back_msh(g, carry):
        wait_group(g, ret2, rsem.at[2, g])
        total[...] += mm(a2t[g], unpack(ret2, g).astype(BF))
        return carry

    lax.fori_loop(0, GROUPS, take_back_msh, 0)
    grad_hidden_bf = (part + mm_nt(total[...].astype(BF), w_send[...])).astype(BF)
    grad_hidden = (cot_bf.astype(F32) + grad_hidden_bf.astype(F32)).astype(BF)
    grad_norm1 = mm_nt(grad_hidden, w_node[...]).astype(BF).astype(F32)
    gathered[...] = norm_backward(grad_norm1, enc_sum, enc_scale).astype(BF)

    def back_enc(g, carry):
        picked = mm(r1[g], gathered[...])
        grad = picked[:MAIN] * d1[g].astype(F32)
        grad_l = fold(picked[MAIN:]) * d1l[g].astype(F32)
        pack_units(back1, g, grad, grad_l)
        send_group(g, back1, ret1, ssem.at[3], rsem.at[3, g], -1)
        d1[g] = grad.astype(BF)
        d1l[g] = grad_l.astype(BF)
        return carry

    lax.fori_loop(0, GROUPS, back_enc, 0)
    grid_sum[...] = jnp.zeros_like(grid_sum)
    total[...] = jnp.zeros_like(total)

    def sum_enc(g, carry):
        both = jnp.concatenate([d1[g], unfold(d1l[g].astype(F32)).astype(BF)], axis=0)
        total[...] += mm(r1t[g], both)
        return carry

    lax.fori_loop(0, GROUPS, sum_enc, 0)
    mesh_part = mm_nt(total[...].astype(BF), w_recv[...]).astype(BF)
    mesh_grad[...] = (grad_hidden.astype(F32) + mesh_part.astype(F32)).astype(BF)

    def take_back_enc(g, carry):
        wait_group(g, ret1, rsem.at[3, g])
        rows, last = unpack_units(ret1, g)
        both = jnp.concatenate([rows.astype(BF), unfold(last).astype(BF)], axis=0)
        grid_sum[...] += mm(a1t[g], both)
        return carry

    lax.fori_loop(0, GROUPS, take_back_enc, 0)
    grid_rows = grid_sum[...]
    grid_grad[...] = mm_nt(grid_rows.astype(BF), w_grid[...]).astype(BF)

    for src, sem in (
        (send1, ssem.at[0]),
        (send2, ssem.at[1]),
        (back2, ssem.at[2]),
        (back1, ssem.at[3]),
        (told, rlsem.at[0]),
        (plane_told, plsem.at[0]),
    ):
        at = src.at[pl.ds(1, src.shape[0] - 1)]
        pltpu.make_async_copy(at, at, sem).wait()


def hand_on(*refs):
    for n in range(3):
        refs[n + 3][...] = refs[n][...]


def body(*args):
    grid_latent, mesh_latent = args[:2]
    args = [v.reshape(1, -1) if n in (7, 10) else v for n, v in enumerate(args)]
    vmem = pl.BlockSpec(memory_space=pltpu.VMEM)
    anywhere = pl.BlockSpec(memory_space=pl.ANY)
    nodes, width = mesh_latent.shape
    grid_nodes = grid_latent.shape[0]

    def block(*shape):
        return pltpu.VMEM(shape, BF)

    scratch = [pltpu.VMEM(v.shape, v.dtype) for v in args]
    scratch += [
        block(PEERS, 9, 4, 128),
        block(PEERS, 9, 4, 128),
        block(PEERS, 48, 128),
        block(PEERS, 48, 128),
        block(PEERS, 48, 128),
        block(PEERS, 48, 128),
        block(PEERS, 9, 4, 128),
        block(PEERS, 9, 4, 128),
        block(GROUPS, ROWS1, grid_nodes),
        block(GROUPS, grid_nodes, ROWS1),
        block(GROUPS, ROWS2, nodes),
        block(GROUPS, nodes, ROWS2),
        block(GROUPS, ROWS1, nodes),
        block(GROUPS, nodes, ROWS1),
        block(GROUPS, ROWS2, nodes),
        block(GROUPS, nodes, ROWS2),
        block(GROUPS, MAIN, width),
        block(GROUPS, LAST, 128),
        block(GROUPS, ROWS2, width),
        block(8, 16, 128),
        block(8, 16, 128),
        block(16, 8, 128),
        block(16, 8, 128),
        block(grid_nodes, width),
        block(nodes, width),
        pltpu.VMEM((nodes, width), F32),
        pltpu.VMEM((nodes, width), F32),
        pltpu.VMEM((grid_nodes, width), F32),
        pltpu.SemaphoreType.DMA((13,)),
        pltpu.SemaphoreType.DMA((4,)),
        pltpu.SemaphoreType.DMA((4, GROUPS)),
        pltpu.SemaphoreType.DMA((2,)),
        pltpu.SemaphoreType.DMA((2,)),
        pltpu.SemaphoreType.REGULAR,
    ]
    results = pl.pallas_call(
        kernel,
        out_shape=(
            jax.ShapeDtypeStruct(mesh_latent.shape, BF),
            jax.ShapeDtypeStruct(grid_latent.shape, BF),
            jax.ShapeDtypeStruct(mesh_latent.shape, BF),
        ),
        in_specs=[anywhere] * 13,
        out_specs=[vmem] * 3,
        scratch_shapes=scratch,
        compiler_params=pltpu.CompilerParams(
            collective_id=0, has_side_effects=True, vmem_limit_bytes=56 << 20
        ),
    )(*args)
    return pl.pallas_call(
        hand_on,
        out_shape=[jax.ShapeDtypeStruct(v.shape, v.dtype) for v in results],
        in_specs=[vmem] * 3,
        out_specs=[vmem] * 3,
    )(*results)


def solution(mesh):
    rows = P(("gx", "gy"), None)
    flat = P(("gx", "gy"))
    placed = (rows, rows, P(), P(), P(), P(), flat, rows, flat, flat, rows, flat, rows)
    return jax.shard_map(
        body, mesh=mesh, in_specs=placed, out_specs=(rows, rows, rows), check_vma=False
    )
```
